128 devices in a mesh: tm: 32 (over z, x, core), height: 4 (over y).
Axes of the slice: x: 4, y: 4, z: 4, core: 2. Of those that a mesh axis runs over, the one named last changes fastest.
Arguments:
- video: bfloat16 [128, 32, 160, 128], P('tm', 'height'), as said below
- conv_weight: bfloat16 [3, 3, 3, 128, 128], replicated, may hold values from -0.109375 to 0.109375
- norm_gain: float32 [128], replicated, may hold values from 0.25 to 1.75
- norm_bias: float32 [128], replicated, may hold values from -3 to 3
- down_weight: bfloat16 [512, 256], replicated, may hold values from -0.25 to 0.25
- length_table: float32 [8, 256], replicated, may hold values from -3 to 3
- keep: int32 [128, 16, 80], P('tm', 'height'), may hold values from 0 to 1, as said below
- run_length: int32 [128, 16, 80], P('tm', 'height'), may hold values from 1 to 8
- owner: int32 [128, 16, 80], P('tm', 'height'), may hold values from 0 to 127
Outputs:
- latent: bfloat16 [128, 16, 80, 256], P('tm', 'height')
- routed: bfloat16 [131072, 256], P(('tm', 'height'))
The draws below stay inside these ranges and needn't reach their ends.
Inputs may be any that keep to these rules, and one draw needn't show every extreme that they name: `keep`: kept patches of one block (the patches of one device) going to one owner number at most 8; in every draw some owner receives exactly 8 from every block. Such per-owner counts may cross devices packed several to a word. `video`: values within -40 to 40.
All inputs are finite; a program needn't handle non-finite values.
Results may differ from the reference program's by a relative error of at most 0.0052.
Values may be sent and summed in bfloat16 or wider, within the bound.
A program may use at most 128 MiB of HBM per device.

```python
import jax
import jax.numpy as jnp
from jax import lax

C = 128
C2 = 256
GROUPS = 32
LMAX = 8
CAP = 8
FT = 4
W = 160
NT = 128
NR = 32
RD2 = 4
NR2 = 16
W2 = 80
TOKS = 1280
OWNERS = 128
OWN_CAP = 1024
N_TM = 32
N_HEIGHT = 4


def route_table(key):
    shape = (NT, NR2, W2)
    frame = lax.broadcasted_iota(jnp.int32, shape, 0)
    row_index = lax.broadcasted_iota(jnp.int32, shape, 1)
    column = lax.broadcasted_iota(jnp.int32, shape, 2)
    block = frame // FT * N_HEIGHT + row_index // RD2
    local = frame % FT * (RD2 * W2) + row_index % RD2 * W2 + column
    first_key, second_key = jax.random.split(key, 2)
    mask_key = jax.random.fold_in(key, 7)
    heavy = jax.random.randint(first_key, (), 0, OWNERS)
    others = jax.random.randint(second_key, shape, 0, OWNERS - 1)
    others = others + (others >= heavy).astype(jnp.int32)
    picked = local % max(TOKS // CAP, 1) == 0
    target = jnp.where(picked, heavy, others).astype(jnp.int32)
    sortkey = ((block * OWNERS + target) * TOKS + local).reshape(-1).astype(jnp.int32)
    order = jnp.argsort(sortkey, stable=True)
    ordered = sortkey[order]
    group = ordered // TOKS
    starts = jnp.searchsorted(group, group, side='left').astype(jnp.int32)
    position = jnp.arange(ordered.shape[0], dtype=jnp.int32) - starts
    ranks = jnp.zeros(ordered.shape, jnp.int32).at[order].set(position).reshape(shape)
    moving = jax.random.randint(mask_key, shape, 0, 4) > 0
    kept = jnp.where((ranks < CAP) & (picked | moving), 1, 0).astype(jnp.int32)
    return (kept, target)


def draw_keep(key, part):
    kept, target = route_table(key)
    return kept


def draw_owner(key, part):
    kept, target = route_table(key)
    return target


def draw_video(key, part):
    key = jax.random.fold_in(key, 5)
    first_key, second_key = jax.random.split(key, 2)
    shape = (NT, NR, W, C)
    height_frac = lax.broadcasted_iota(jnp.float32, (1, NR, 1, 1), 1) / max(NR - 1, 1)
    column_frac = jax.random.uniform(second_key, (1, 1, W, 1), jnp.float32)
    base = jnp.clip(jax.random.normal(first_key, shape, jnp.float32), -4.0, 4.0)
    scale = jnp.power(10.0, 0.5 * height_frac) * jnp.power(10.0, 0.5 * column_frac)
    return (base * scale).astype(jnp.bfloat16)


def plant(array, rng, smallest, top_value):
    dims = array.shape
    index_at = [jax.random.randint(jax.random.fold_in(rng, axis), (), 0, dims[axis]) for axis in range(len(dims))]
    array = array.at[tuple(index_at)].set(smallest)
    longest = dims.index(max(dims))
    index_at[longest] = (index_at[longest] + 1) % dims[longest]
    return array.at[tuple(index_at)].set(top_value)


def bell_draw(stream_key, extent, scale, reach, kind=jnp.bfloat16):
    drawn = jax.random.normal(stream_key, extent, jnp.float32) * scale
    return jnp.minimum(jnp.maximum(drawn, -reach), reach).astype(kind)


def setup_inputs(seed: int = 0) -> dict:
    key_of = jax.random.split(jax.random.key(seed), 10)
    return {
        "video": draw_video(jax.random.fold_in(key_of[9], 71), 0),
        "conv_weight": bell_draw(key_of[1], (3, 3, 3, C, C), (27 * C) ** -0.5, 0.109375),
        "norm_gain": jnp.clip(1.0 + 0.15 * jax.random.normal(key_of[2], (C,), jnp.float32), 0.25, 1.75),
        "norm_bias": bell_draw(key_of[3], (C,), 0.5, 3.0, jnp.float32),
        "down_weight": bell_draw(key_of[4], (4 * C, C2), (4 * C) ** -0.5, 0.25),
        "length_table": bell_draw(key_of[5], (LMAX, C2), 0.5, 3.0, jnp.float32),
        "keep": draw_keep(jax.random.fold_in(key_of[9], 71), 0),
        "run_length": plant(jax.random.randint(key_of[7], (NT, NR2, W2), 1, LMAX + 1), jax.random.fold_in(key_of[7], 1), 1, LMAX).astype(jnp.int32),
        "owner": draw_owner(jax.random.fold_in(key_of[9], 71), 0),
    }


EPSILON = 1e-06

def causal_block(window, conv_weight):
    result = lax.conv_general_dilated(window.astype(jnp.float32)[None], conv_weight.astype(jnp.float32), (1, 1, 1), ((0, 0), (1, 1), (1, 1)), dimension_numbers=('NDHWC', 'DHWIO', 'NDHWC'), precision=lax.Precision.HIGHEST)
    return result[0]

def reference(video, conv_weight, norm_gain, norm_bias, down_weight, length_table, keep, run_length, owner):
    padded = jnp.concatenate([jnp.zeros((2, NR, W, C), jnp.bfloat16), video], axis=0)

    def one_block(number):
        window = lax.dynamic_slice_in_dim(padded, (number * FT).astype(jnp.int32), FT + 2, 0)
        return causal_block(window, conv_weight)
    hidden = lax.map(one_block, jnp.arange(N_TM, dtype=jnp.int32)).reshape(NT, NR, W, C)
    grouped = hidden.reshape(NT, NR * W, GROUPS, C // GROUPS)
    count = NR * W * (C // GROUPS)
    average = lax.optimization_barrier(jnp.sum(grouped, axis=(1, 3))) / count
    squares = lax.optimization_barrier(jnp.sum(grouped * grouped, axis=(1, 3))) / count
    spread = squares - average * average
    normed = (grouped - average[:, None, :, None]) * lax.rsqrt(spread + EPSILON)[:, None, :, None]
    normed = normed.reshape(NT, NR, W, C) * norm_gain + norm_bias
    active = jax.nn.silu(normed).astype(jnp.bfloat16)
    patched = active.reshape(NT, NR2, 2, W2, 2, C).transpose(0, 1, 3, 2, 4, 5).reshape(NT * NR2 * W2, 4 * C)
    latent = jnp.dot(patched, down_weight, preferred_element_type=jnp.float32).astype(jnp.bfloat16)
    values = (latent.astype(jnp.float32) + length_table[run_length.reshape(-1) - 1]).astype(jnp.bfloat16)
    frame = lax.broadcasted_iota(jnp.int32, (NT, NR2, W2), 0)
    row_index = lax.broadcasted_iota(jnp.int32, (NT, NR2, W2), 1)
    column = lax.broadcasted_iota(jnp.int32, (NT, NR2, W2), 2)
    block = frame // FT * N_HEIGHT + row_index // RD2
    local = frame % FT * (RD2 * W2) + row_index % RD2 * W2 + column
    sortkey = jnp.where(keep == 1, owner * (OWNERS * TOKS) + block * TOKS + local, OWNERS * OWNERS * TOKS).reshape(-1).astype(jnp.int32)
    order = jnp.argsort(sortkey, stable=True)
    ordered = sortkey[order]
    target = (ordered // (OWNERS * TOKS)).astype(jnp.int32)
    starts = jnp.searchsorted(target, target, side='left').astype(jnp.int32)
    position = jnp.arange(ordered.shape[0], dtype=jnp.int32) - starts
    destination = jnp.where(target < OWNERS, target * OWN_CAP + position, OWNERS * OWN_CAP).astype(jnp.int32)
    routed = jnp.zeros((OWNERS * OWN_CAP, C2), jnp.bfloat16).at[destination].set(values[order], mode='drop')
    return (latent.reshape(NT, NR2, W2, C2), routed)
```

```python
import functools

import jax
import jax.numpy as jnp
from jax import lax
from jax.experimental import pallas as pl
from jax.experimental.pallas import tpu as pltpu
from jax.sharding import PartitionSpec as P

GROUPS = 32
LMAX = 8
CAP = 8
EPSILON = 1e-06
LANES = 128
EMPTY = 2.0**127
LIMIT = 2.0**126
MESH = pl.DeviceIdType.MESH
F32 = jnp.float32
BF16 = jnp.bfloat16


def dot(a, b):
    return jnp.dot(a, b, preferred_element_type=F32)


def dot_t(a, b, precision=None):
    return lax.dot_general(
        a, b, (((1,), (1,)), ((), ())), preferred_element_type=F32, precision=precision
    )


def iota(shape, dim):
    return lax.broadcasted_iota(jnp.int32, shape, dim)


def onehot(mask):
    return jnp.where(mask, 1.0, 0.0).astype(BF16)


def encode_kernel(
    ntm, nh, shapes,
    video, weight, gain, bias, down, table, keep, run, owner,
    latent_out, payload_out,
    xbuf, wbuf, hidden, stat, codes, routes, extra, lat, pay,
    in_sem, w_sem, halo_send, halo_recv, stat_send, stat_recv, out_sem,
):
    frames, rows, cols, chans, width = shapes
    half_rows, half_cols = rows // 2, cols // 2
    toks = frames * half_rows * half_cols
    owners = ntm * nh
    slots = owners * CAP
    me_t, me_h = lax.axis_index("tm"), lax.axis_index("height")
    next_t, last_t = lax.rem(me_t + 1, ntm), lax.rem(me_t + ntm - 1, ntm)
    up, down_h = lax.rem(me_h + nh - 1, nh), lax.rem(me_h + 1, nh)
    peers = [lax.rem(me_h + k, nh) for k in range(1, nh)]

    own = pltpu.make_async_copy(
        video, xbuf.at[pl.ds(2, frames), pl.ds(1, rows)], in_sem
    )
    own.start()
    wcopies = [
        pltpu.make_async_copy(
            weight.at[:, e], wbuf.at[:, :, pl.ds(e * chans, chans)], w_sem.at[e]
        )
        for e in range(3)
    ]
    for copy in wcopies:
        copy.start()

    barrier = pltpu.get_barrier_semaphore()
    sources = [(last_t, me_h), (last_t, up), (last_t, down_h)] + [(me_t, h) for h in peers]
    for t, h in sources:
        pl.semaphore_signal(
            barrier, inc=1, device_id={"tm": t, "height": h}, device_id_type=MESH
        )
    pl.semaphore_wait(barrier, len(sources))

    def halo(k, src, dst, t, h):
        return pltpu.make_async_remote_copy(
            src_ref=src, dst_ref=dst, send_sem=halo_send.at[k], recv_sem=halo_recv.at[k],
            device_id={"tm": t, "height": h}, device_id_type=MESH,
        )

    own_rows = pl.ds(1, rows)
    to_up = halo(0, video.at[:, 0], xbuf.at[pl.ds(2, frames), rows + 1], me_t, up)
    to_down = halo(1, video.at[:, rows - 1], xbuf.at[pl.ds(2, frames), 0], me_t, down_h)
    late = halo(2, video.at[frames - 1], xbuf.at[1, own_rows], next_t, me_h)
    early = halo(3, video.at[frames - 2], xbuf.at[0, own_rows], next_t, me_h)
    pair = pl.ds(frames - 2, 2)
    corner_up = halo(4, video.at[pair, 0], xbuf.at[pl.ds(0, 2), rows + 1], next_t, up)
    corner_down = halo(5, video.at[pair, rows - 1], xbuf.at[pl.ds(0, 2), 0], next_t, down_h)
    for copy in (late, to_up, to_down, early, corner_up, corner_down):
        copy.start()

    codes[...] = jnp.zeros(codes.shape, F32)
    for t in range(frames):
        kept = keep[t] == 1
        where_to = jnp.where(kept, owner[t], owners)
        codes[0, pl.ds(t * half_rows, half_rows), pl.ds(0, half_cols)] = where_to.astype(F32)
        codes[1, pl.ds(t * half_rows, half_rows), pl.ds(0, half_cols)] = (
            run[t] - 1
        ).astype(F32)
    lines = frames * half_rows
    wide = codes.shape[2]
    spread_at = onehot(iota((wide, toks), 0) == lax.rem(iota((wide, toks), 1), half_cols))
    mine = iota((lines, toks), 0) == iota((lines, toks), 1) // half_cols
    code = jnp.sum(
        jnp.where(mine, dot(codes[0].astype(BF16), spread_at), 0.0), axis=0, keepdims=True
    )
    length = jnp.sum(
        jnp.where(mine, dot(codes[1].astype(BF16), spread_at), 0.0), axis=0, keepdims=True
    )
    code_i, length_i = code.astype(jnp.int32), length.astype(jnp.int32)
    member = iota((owners, toks), 0) == code_i
    before_lane = onehot(iota((LANES, LANES), 0) < iota((LANES, LANES), 1))
    carry = jnp.zeros((owners, 1), F32)
    for k in range(toks // LANES):
        at = slice(k * LANES, (k + 1) * LANES)
        block = jnp.where(member[:, at], 1.0, 0.0)
        ahead = dot(block.astype(BF16), before_lane) + carry
        carry = carry + jnp.sum(block, axis=1, keepdims=True)
        rank = jnp.sum(ahead * block, axis=0, keepdims=True).astype(jnp.int32)
        slot = jnp.where(code_i[:, at] < owners, code_i[:, at] * CAP + rank, -1)
        routes[:, at] = onehot(iota((slots, LANES), 0) == slot)
    lanes_t = 4 * LMAX
    line = iota((lanes_t, toks), 0)
    which = onehot((lax.rem(line, LMAX) == length_i) | (line >= 3 * LMAX))
    part0 = table[...].astype(BF16)
    rest = table[...] - part0.astype(F32)
    part1 = rest.astype(BF16)
    part2 = (rest - part1.astype(F32)).astype(BF16)
    parts = jnp.concatenate(
        [part0.astype(F32), part1.astype(F32), part2.astype(F32), jnp.zeros((LMAX, width), F32)],
        axis=0,
    ).astype(BF16)
    picked = dot_t(routes[...], which)
    added = dot(picked.astype(BF16), parts)
    extra[...] = jnp.where(picked[:, 3 * LMAX : 3 * LMAX + 1] > 0.5, added, EMPTY)

    for copy in wcopies:
        copy.wait()
    own.wait()

    first = iota((1, cols, chans), 1) == 0
    final = iota((1, cols, chans), 1) == cols - 1

    def convolve(t, r0, count):
        window = jnp.concatenate(
            [
                xbuf[t + a, pl.ds(r0 + b, count)].reshape(count * cols, chans)
                for a in range(3)
                for b in range(3)
            ],
            axis=1,
        )
        taps = dot(window, wbuf[...].reshape(9 * chans, 3 * chans))
        left = pltpu.roll(taps[:, :chans], 1, 0).reshape(count, cols, chans)
        right = pltpu.roll(taps[:, 2 * chans :], count * cols - 1, 0).reshape(count, cols, chans)
        out = taps[:, chans : 2 * chans].reshape(count, cols, chans)
        out = out + jnp.where(first, 0.0, left) + jnp.where(final, 0.0, right)
        hidden[t, pl.ds(r0, count)] = out
        tiles = out.reshape(count * cols // 8, 8, chans)
        stat[me_h, t, pl.ds(0, 8)] += jnp.sum(tiles, axis=0)
        stat[me_h, t, pl.ds(8, 8)] += jnp.sum(tiles * tiles, axis=0)

    def clear_rows(at, count):
        @pl.when(me_h == 0)
        def _():
            xbuf[pl.ds(at, count), 0] = jnp.zeros((count, cols, chans), BF16)

        @pl.when(me_h == nh - 1)
        def _():
            xbuf[pl.ds(at, count), rows + 1] = jnp.zeros((count, cols, chans), BF16)

    def clear_frame(at):
        @pl.when(me_t == 0)
        def _():
            xbuf[at] = jnp.zeros((rows + 2, cols, chans), BF16)

    def stat_copy(t, k):
        return pltpu.make_async_remote_copy(
            src_ref=stat.at[me_h, t], dst_ref=stat.at[me_h, t],
            send_sem=stat_send.at[t, k], recv_sem=stat_recv.at[t, me_h],
            device_id={"tm": me_t, "height": peers[k]}, device_id_type=MESH,
        )

    def stat_arrival(t, k):
        return pltpu.make_async_remote_copy(
            src_ref=stat.at[peers[k], t], dst_ref=stat.at[peers[k], t],
            send_sem=stat_send.at[t, k], recv_sem=stat_recv.at[t, peers[k]],
            device_id={"tm": me_t, "height": peers[k]}, device_id_type=MESH,
        )

    step = 2

    def frame_conv(t):
        stat[me_h, t] = jnp.zeros(stat.shape[2:], F32)

        def some(i, _):
            convolve(t, i * step, step)
            return 0

        lax.fori_loop(0, rows // step, some, 0)
        for k in range(nh - 1):
            stat_copy(t, k).start()

    group_of = chans // GROUPS
    same = jnp.where(
        iota((chans, chans), 0) // group_of == iota((chans, chans), 1) // group_of, 1.0, 0.0
    )
    count = rows * nh * cols * group_of

    def finish(t):
        for k in range(nh - 1):
            stat_arrival(t, k).wait_recv()
        summed = jnp.sum(stat[:, t], axis=0).reshape(2, 8, chans)
        summed = jnp.sum(summed, axis=1)
        pads = jnp.concatenate([summed, jnp.zeros((6, chans), F32)], axis=0)
        grouped = jnp.dot(
            pads, same, preferred_element_type=F32, precision=lax.Precision.HIGHEST
        ) / count
        average, squares = grouped[0:1], grouped[1:2]
        spread = squares - average * average
        scale = lax.rsqrt(spread + EPSILON) * gain[...]

        def act(r, b):
            h = hidden[t, r, pl.ds(b, half_cols, stride=2), :]
            v = 0.5 * ((h - average) * scale + bias[...])
            return (v * (1.0 + jnp.tanh(v))).astype(BF16)

        for i in range(half_rows):
            merged = jnp.concatenate(
                [act(2 * i + a, b) for a in range(2) for b in range(2)], axis=1
            )
            lat[t * half_rows + i] = dot(merged, down[...]).astype(BF16)
        pltpu.make_async_copy(
            lat.at[pl.ds(t * half_rows, half_rows)], latent_out.at[t], out_sem.at[t]
        ).start()

    to_up.wait_recv()
    to_down.wait_recv()
    clear_rows(2, frames)
    for t in range(frames - 1, 1, -1):
        frame_conv(t)
    late.wait_recv()
    early.wait_recv()
    corner_up.wait_recv()
    corner_down.wait_recv()
    clear_rows(0, 2)
    clear_frame(0)
    clear_frame(1)
    frame_conv(1)
    frame_conv(0)
    for t in range(frames - 1, -1, -1):
        finish(t)
    out = dot(routes[...], lat[...].reshape(toks, width)) + extra[...]
    sides = [
        out[:, k * LANES : (k + 1) * LANES].reshape(owners, CAP, LANES)
        for k in range(width // LANES)
    ]
    pay[...] = jnp.concatenate(sides, axis=1).astype(BF16)
    leave = pltpu.make_async_copy(pay, payload_out, out_sem.at[frames])
    leave.start()
    for copy in (late, to_up, to_down, early, corner_up, corner_down):
        copy.wait_send()
    for t in range(frames):
        for k in range(nh - 1):
            stat_copy(t, k).wait_send()
        pltpu.make_async_copy(
            lat.at[pl.ds(t * half_rows, half_rows)], latent_out.at[t], out_sem.at[t]
        ).wait()
    leave.wait()


def compact(arrived, owners, width):
    slots = owners * CAP
    block = min(LANES, slots)
    tall = arrived.astype(F32)
    sides = [
        tall[:, k * CAP : (k + 1) * CAP].reshape(slots, LANES) for k in range(width // LANES)
    ]
    rows = jnp.concatenate(sides, axis=1).astype(BF16)
    pick = onehot(iota((8, LANES), 1) == 0)
    lead = dot_t(pick, sides[0].astype(BF16))
    ahead_of = onehot(iota((block, block), 0) < iota((block, block), 1))
    carry = jnp.zeros((8, 1), F32)
    places = []
    for k in range(slots // block):
        valid = jnp.where(lead[:, k * block : (k + 1) * block] < LIMIT, 1.0, 0.0)
        place = dot(valid.astype(BF16), ahead_of) + carry
        carry = carry + jnp.sum(valid, axis=1, keepdims=True)
        places.append(jnp.where(valid > 0.5, place, -1.0)[0:1].astype(jnp.int32))
    chosen = jnp.concatenate(
        [onehot(iota((slots, block), 0) == place) for place in places], axis=1
    )
    return dot(chosen, rows).astype(BF16)


def compact_kernel(owners, width, arrived, routed):
    routed[...] = compact(arrived[...], owners, width)


def on_device(
    ntm, nh, video, conv_weight, norm_gain, norm_bias, down_weight, length_table, keep, run_length, owner
):
    frames, rows, cols, chans = video.shape
    width = down_weight.shape[1]
    half_rows, half_cols = rows // 2, cols // 2
    toks = frames * half_rows * half_cols
    owners = ntm * nh
    slots = owners * CAP
    any_spec = pl.BlockSpec(memory_space=pl.ANY)
    vmem = pl.BlockSpec(memory_space=pltpu.VMEM)
    tiles = CAP * width // LANES
    latent, payload = pl.pallas_call(
        functools.partial(encode_kernel, ntm, nh, (frames, rows, cols, chans, width)),
        out_shape=(
            jax.ShapeDtypeStruct((frames, half_rows, half_cols, width), BF16),
            jax.ShapeDtypeStruct((owners, tiles, LANES), BF16),
        ),
        in_specs=[any_spec, any_spec] + [vmem] * 7,
        out_specs=(any_spec, any_spec),
        scratch_shapes=[
            pltpu.VMEM((frames + 2, rows + 2, cols, chans), BF16),
            pltpu.VMEM((9, chans, 3 * chans), BF16),
            pltpu.VMEM((frames, rows, cols, chans), F32),
            pltpu.VMEM((nh, frames, 16, chans), F32),
            pltpu.VMEM((2, frames * half_rows, LANES), F32),
            pltpu.VMEM((slots, toks), BF16),
            pltpu.VMEM((slots, width), F32),
            pltpu.VMEM((frames * half_rows, half_cols, width), BF16),
            pltpu.VMEM((owners, tiles, LANES), BF16),
            pltpu.SemaphoreType.DMA,
            pltpu.SemaphoreType.DMA((3,)),
            pltpu.SemaphoreType.DMA((6,)),
            pltpu.SemaphoreType.DMA((6,)),
            pltpu.SemaphoreType.DMA((frames, nh - 1)),
            pltpu.SemaphoreType.DMA((frames, nh)),
            pltpu.SemaphoreType.DMA((frames + 1,)),
        ],
        compiler_params=pltpu.CompilerParams(
            collective_id=0, has_side_effects=True, vmem_limit_bytes=48 * 1024 * 1024
        ),
        name="encode",
    )(
        video,
        conv_weight.reshape(9, 3, chans, chans),
        norm_gain.reshape(1, chans),
        norm_bias.reshape(1, chans),
        down_weight,
        length_table,
        keep,
        run_length,
        owner,
    )
    arrived = lax.all_to_all(
        payload, ("tm", "height"), split_axis=0, concat_axis=0, tiled=True
    )
    routed = pl.pallas_call(
        functools.partial(compact_kernel, owners, width),
        out_shape=jax.ShapeDtypeStruct((slots, width), BF16),
        in_specs=[vmem],
        out_specs=vmem,
        compiler_params=pltpu.CompilerParams(vmem_limit_bytes=48 * 1024 * 1024),
        name="compact",
    )(arrived)
    return latent, routed


def solution(mesh):
    return jax.shard_map(
        functools.partial(on_device, mesh.shape["tm"], mesh.shape["height"]),
        mesh=mesh,
        in_specs=(
            P("tm", "height", None, None),
            P(),
            P(),
            P(),
            P(),
            P(),
            P("tm", "height", None),
            P("tm", "height", None),
            P("tm", "height", None),
        ),
        out_specs=(P("tm", "height", None, None), P(("tm", "height"), None)),
        check_vma=False,
    )
```

```python
import functools

import jax
import jax.numpy as jnp
from jax import lax
from jax.experimental import pallas as pl
from jax.experimental.pallas import tpu as pltpu
from jax.sharding import PartitionSpec as P

GROUPS = 32
LMAX = 8
CAP = 8
EPSILON = 1e-06
LANES = 128
EMPTY = 2.0**127
LIMIT = 2.0**126
MESH = pl.DeviceIdType.MESH
F32 = jnp.float32
BF16 = jnp.bfloat16


def dot(a, b):
    return jnp.dot(a, b, preferred_element_type=F32)


def dot_t(a, b, precision=None):
    return lax.dot_general(
        a, b, (((1,), (1,)), ((), ())), preferred_element_type=F32, precision=precision
    )


def iota(shape, dim):
    return lax.broadcasted_iota(jnp.int32, shape, dim)


def onehot(mask):
    return jnp.where(mask, 1.0, 0.0).astype(BF16)


def encode_kernel(
    ntm, nh, shapes, ways,
    video_in, weight_in, gain_in, bias_in, down_in, table_in, keep_in, run_in, owner_in,
    latent_out, arrived,
    xbuf, wpair, wlast, gain, bias, down, table, keep, run, owner,
    hidden, stat, codes, routes, extra, lat, pay,
    in_sem, halo_send, halo_recv, stat_send, stat_recv, ready, out_sem, go_sem, come_sem,
):
    frames, rows, cols, chans, width = shapes
    half_rows, half_cols = rows // 2, cols // 2
    toks = frames * half_rows * half_cols
    owners = ntm * nh
    slots = owners * CAP
    me_t, me_h = lax.axis_index("tm"), lax.axis_index("height")
    me = me_t * nh + me_h
    next_t, last_t = lax.rem(me_t + 1, ntm), lax.rem(me_t + ntm - 1, ntm)
    up, down_h = lax.rem(me_h + nh - 1, nh), lax.rem(me_h + 1, nh)
    peers = [lax.rem(me_h + k, nh) for k in range(1, nh)]

    fast, slow = ways
    plane, line = me_t // fast, lax.rem(me_t, fast)
    rounds = [
        [(me_t, h) for h in peers],
        [(plane * fast + lax.rem(line + k, fast), me_h) for k in range(1, fast)],
        [(lax.rem(plane + k, slow) * fast + line, me_h) for k in range(1, slow)],
    ]
    sources = [(last_t, me_h), (last_t, up), (last_t, down_h)]
    sources += [target for group in rounds for target in group]
    barrier = pltpu.get_barrier_semaphore()
    for t, h in sources:
        pl.semaphore_signal(
            barrier, inc=1, device_id={"tm": t, "height": h}, device_id_type=MESH
        )

    loads = [
        (keep_in, keep), (run_in, run), (owner_in, owner), (table_in, table),
        (video_in, xbuf.at[pl.ds(2, frames), pl.ds(1, rows)]),
        (weight_in.at[:, :, 0], wpair.at[:, :, :, pl.ds(0, chans)]),
        (weight_in.at[:, :, 1], wpair.at[:, :, :, pl.ds(chans, chans)]),
        (weight_in.at[:, :, 2], wlast.at[:, pl.ds(0, 3), :, pl.ds(0, chans)]),
        (weight_in.at[:, :, 2], wlast.at[:, pl.ds(1, 3), :, pl.ds(chans, chans)]),
        (down_in, down), (gain_in, gain), (bias_in, bias),
    ]
    loads = [
        pltpu.make_async_copy(src, dst, in_sem.at[k]) for k, (src, dst) in enumerate(loads)
    ]
    for copy in loads:
        copy.start()
    wlast[:, 3, :, pl.ds(0, chans)] = jnp.zeros((3, chans, chans), BF16)
    wlast[:, 0, :, pl.ds(chans, chans)] = jnp.zeros((3, chans, chans), BF16)
    pl.semaphore_wait(barrier, len(sources))

    def halo(k, src, dst, t, h):
        return pltpu.make_async_remote_copy(
            src_ref=src, dst_ref=dst, send_sem=halo_send.at[k], recv_sem=halo_recv.at[k],
            device_id={"tm": t, "height": h}, device_id_type=MESH,
        )

    own_rows = pl.ds(1, rows)
    to_up = halo(0, video_in.at[:, 0], xbuf.at[pl.ds(2, frames), rows + 1], me_t, up)
    to_down = halo(1, video_in.at[:, rows - 1], xbuf.at[pl.ds(2, frames), 0], me_t, down_h)
    late = halo(2, video_in.at[frames - 1], xbuf.at[1, own_rows], next_t, me_h)
    early = halo(3, video_in.at[frames - 2], xbuf.at[0, own_rows], next_t, me_h)
    pair = pl.ds(frames - 2, 2)
    corner_up = halo(4, video_in.at[pair, 0], xbuf.at[pl.ds(0, 2), rows + 1], next_t, up)
    corner_down = halo(5, video_in.at[pair, rows - 1], xbuf.at[pl.ds(0, 2), 0], next_t, down_h)
    halos = (late, to_up, to_down, early, corner_up, corner_down)
    for copy in halos:
        copy.start()

    def tell(k):
        for t, h in rounds[k]:
            pl.semaphore_signal(
                ready.at[k], inc=1, device_id={"tm": t, "height": h}, device_id_type=MESH
            )

    def hear(k):
        if rounds[k]:
            pl.semaphore_wait(ready.at[k], len(rounds[k]))

    tell(0)
    for copy in loads[:4]:
        copy.wait()
    codes[...] = jnp.zeros(codes.shape, F32)
    for t in range(frames):
        kept = keep[t] == 1
        where_to = jnp.where(kept, owner[t], owners)
        codes[0, pl.ds(t * half_rows, half_rows), pl.ds(0, half_cols)] = where_to.astype(F32)
        codes[1, pl.ds(t * half_rows, half_rows), pl.ds(0, half_cols)] = (
            run[t] - 1
        ).astype(F32)
    lines = frames * half_rows
    wide = codes.shape[2]
    spread_at = onehot(iota((wide, toks), 0) == lax.rem(iota((wide, toks), 1), half_cols))
    mine = iota((lines, toks), 0) == iota((lines, toks), 1) // half_cols
    code = jnp.sum(
        jnp.where(mine, dot(codes[0].astype(BF16), spread_at), 0.0), axis=0, keepdims=True
    )
    length = jnp.sum(
        jnp.where(mine, dot(codes[1].astype(BF16), spread_at), 0.0), axis=0, keepdims=True
    )
    code_i, length_i = code.astype(jnp.int32), length.astype(jnp.int32)
    member = iota((owners, toks), 0) == code_i
    before_lane = onehot(iota((LANES, LANES), 0) < iota((LANES, LANES), 1))
    carry = jnp.zeros((owners, 1), F32)
    for k in range(toks // LANES):
        at = slice(k * LANES, (k + 1) * LANES)
        block = jnp.where(member[:, at], 1.0, 0.0)
        ahead = dot(block.astype(BF16), before_lane) + carry
        carry = carry + jnp.sum(block, axis=1, keepdims=True)
        rank = jnp.sum(ahead * block, axis=0, keepdims=True).astype(jnp.int32)
        slot = jnp.where(code_i[:, at] < owners, code_i[:, at] * CAP + rank, -1)
        routes[:, at] = onehot(iota((slots, LANES), 0) == slot)
    lanes_t = 4 * LMAX
    row_of = iota((lanes_t, toks), 0)
    which = onehot((lax.rem(row_of, LMAX) == length_i) | (row_of >= 3 * LMAX))
    part0 = table[...].astype(BF16)
    rest = table[...] - part0.astype(F32)
    part1 = rest.astype(BF16)
    part2 = (rest - part1.astype(F32)).astype(BF16)
    parts = jnp.concatenate(
        [part0.astype(F32), part1.astype(F32), part2.astype(F32), jnp.zeros((LMAX, width), F32)],
        axis=0,
    ).astype(BF16)
    picked = dot_t(routes[...], which)
    added = dot(picked.astype(BF16), parts)
    extra[...] = jnp.where(picked[:, 3 * LMAX : 3 * LMAX + 1] > 0.5, added, EMPTY)

    for copy in loads[4:]:
        copy.wait()
    hear(0)
    tell(1)

    first = iota((1, cols, chans), 1) == 0
    final = iota((1, cols, chans), 1) == cols - 1

    def convolve(t, r0, count):
        half = count // 2
        window = jnp.concatenate(
            [
                xbuf[t + a, pl.ds(r0 + b, count)].reshape(count * cols, chans)
                for a in range(3)
                for b in range(3)
            ],
            axis=1,
        )
        taps = dot(window, wpair[...].reshape(9 * chans, 2 * chans))
        left = pltpu.roll(taps[:, :chans], 1, 0).reshape(count, cols, chans)
        out = taps[:, chans:].reshape(count, cols, chans) + jnp.where(first, 0.0, left)
        window = jnp.concatenate(
            [
                jnp.concatenate([xbuf[t + a, r0 + b + 2 * i] for i in range(half)], axis=0)
                for a in range(3)
                for b in range(4)
            ],
            axis=1,
        )
        taps = dot(window, wlast[...].reshape(12 * chans, 2 * chans))
        right = jnp.concatenate(
            [
                pltpu.roll(taps[:, k * chans : (k + 1) * chans], half * cols - 1, 0).reshape(
                    half, 1, cols, chans
                )
                for k in range(2)
            ],
            axis=1,
        ).reshape(count, cols, chans)
        out = out + jnp.where(final, 0.0, right)
        hidden[t, pl.ds(r0, count)] = out
        tiles = out.reshape(count * cols // 8, 8, chans)
        stat[me_h, t, pl.ds(0, 8)] = jnp.sum(tiles, axis=0)
        stat[me_h, t, pl.ds(8, 8)] = jnp.sum(tiles * tiles, axis=0)

    def clear_rows(at, count):
        @pl.when(me_h == 0)
        def _():
            xbuf[pl.ds(at, count), 0] = jnp.zeros((count, cols, chans), BF16)

        @pl.when(me_h == nh - 1)
        def _():
            xbuf[pl.ds(at, count), rows + 1] = jnp.zeros((count, cols, chans), BF16)

    def stat_copy(t, k):
        return pltpu.make_async_remote_copy(
            src_ref=stat.at[me_h, t], dst_ref=stat.at[me_h, t],
            send_sem=stat_send.at[t, k], recv_sem=stat_recv.at[t, me_h],
            device_id={"tm": me_t, "height": peers[k]}, device_id_type=MESH,
        )

    def stat_arrival(t, k):
        return pltpu.make_async_remote_copy(
            src_ref=stat.at[peers[k], t], dst_ref=stat.at[peers[k], t],
            send_sem=stat_send.at[t, k], recv_sem=stat_recv.at[t, peers[k]],
            device_id={"tm": me_t, "height": peers[k]}, device_id_type=MESH,
        )

    def frame_conv(t):
        convolve(t, 0, rows)
        for k in range(nh - 1):
            stat_copy(t, k).start()

    group_of = chans // GROUPS
    same = jnp.where(
        iota((chans, chans), 0) // group_of == iota((chans, chans), 1) // group_of, 1.0, 0.0
    )
    count = rows * nh * cols * group_of

    def finish(t):
        for k in range(nh - 1):
            stat_arrival(t, k).wait_recv()
        summed = jnp.sum(stat[:, t], axis=0).reshape(2, 8, chans)
        summed = jnp.sum(summed, axis=1)
        pads = jnp.concatenate([summed, jnp.zeros((6, chans), F32)], axis=0)
        grouped = jnp.dot(
            pads, same, preferred_element_type=F32, precision=lax.Precision.HIGHEST
        ) / count
        average, squares = grouped[0:1], grouped[1:2]
        spread = squares - average * average
        scale = lax.rsqrt(spread + EPSILON) * gain[...]

        def act(r, b):
            h = hidden[t, r, pl.ds(b, half_cols, stride=2), :]
            v = 0.5 * ((h - average) * scale + bias[...])
            return (v * (1.0 + jnp.tanh(v))).astype(BF16)

        merged = jnp.concatenate(
            [
                jnp.concatenate(
                    [act(2 * i + a, b) for a in range(2) for b in range(2)], axis=1
                )
                for i in range(half_rows)
            ],
            axis=0,
        )
        lat[pl.ds(t * half_rows, half_rows)] = (
            dot(merged, down[...]).astype(BF16).reshape(half_rows, half_cols, width)
        )
        latent_copy(t).start()

    def latent_copy(t):
        return pltpu.make_async_copy(
            lat.at[pl.ds(t * half_rows, half_rows)], latent_out.at[t], out_sem.at[t]
        )

    to_up.wait_recv()
    to_down.wait_recv()
    clear_rows(2, frames)
    for t in range(frames - 1, 1, -1):
        frame_conv(t)
    hear(1)
    tell(2)
    late.wait_recv()
    corner_up.wait_recv()
    corner_down.wait_recv()
    early.wait_recv()
    clear_rows(0, 2)

    @pl.when(me_t == 0)
    def _():
        xbuf[0:2] = jnp.zeros((2, rows + 2, cols, chans), BF16)

    frame_conv(1)
    frame_conv(0)
    hear(2)
    for t in range(frames - 1, -1, -1):
        finish(t)

    out = dot(routes[...], lat[...].reshape(toks, width)) + extra[...]
    sides = [
        out[:, k * LANES : (k + 1) * LANES].reshape(owners, CAP, LANES)
        for k in range(width // LANES)
    ]
    pay[...] = jnp.concatenate(sides, axis=1).astype(BF16)
    mine_copy = pltpu.make_async_copy(pay.at[me], arrived.at[me], out_sem.at[frames])
    mine_copy.start()

    def send(k, _):
        to = lax.rem(me + k, owners)
        pltpu.make_async_remote_copy(
            src_ref=pay.at[to], dst_ref=arrived.at[me], send_sem=go_sem, recv_sem=come_sem,
            device_id={"tm": to // nh, "height": lax.rem(to, nh)}, device_id_type=MESH,
        ).start()
        return 0

    lax.fori_loop(1, owners, send, 0)
    for copy in halos:
        copy.wait_send()
    for t in range(frames):
        for k in range(nh - 1):
            stat_copy(t, k).wait_send()
        latent_copy(t).wait()
    mine_copy.wait()
    others = pl.ds(0, owners - 1)
    pltpu.make_async_copy(pay.at[others], arrived.at[others], come_sem).wait()
    pltpu.make_async_copy(pay.at[others], arrived.at[others], go_sem).wait()


def compact(arrived, owners, width):
    slots = owners * CAP
    block = min(LANES, slots)
    tall = arrived.astype(F32)
    sides = [
        tall[:, k * CAP : (k + 1) * CAP].reshape(slots, LANES) for k in range(width // LANES)
    ]
    rows = jnp.concatenate(sides, axis=1).astype(BF16)
    pick = onehot(iota((8, LANES), 1) == 0)
    lead = dot_t(pick, sides[0].astype(BF16))
    ahead_of = onehot(iota((block, block), 0) < iota((block, block), 1))
    carry = jnp.zeros((8, 1), F32)
    places = []
    for k in range(slots // block):
        valid = jnp.where(lead[:, k * block : (k + 1) * block] < LIMIT, 1.0, 0.0)
        place = dot(valid.astype(BF16), ahead_of) + carry
        carry = carry + jnp.sum(valid, axis=1, keepdims=True)
        places.append(jnp.where(valid > 0.5, place, -1.0)[0:1].astype(jnp.int32))
    chosen = jnp.concatenate(
        [onehot(iota((slots, block), 0) == place) for place in places], axis=1
    )
    return dot(chosen, rows).astype(BF16)


def compact_kernel(owners, width, arrived, latent_in, routed, latent_out, sem):
    copy = pltpu.make_async_copy(latent_in, latent_out, sem)
    copy.start()
    routed[...] = compact(arrived[...], owners, width)
    copy.wait()


def on_device(
    ntm, nh, video, conv_weight, norm_gain, norm_bias, down_weight, length_table, keep, run_length, owner
):
    frames, rows, cols, chans = video.shape
    width = down_weight.shape[1]
    half_rows, half_cols = rows // 2, cols // 2
    toks = frames * half_rows * half_cols
    owners = ntm * nh
    slots = owners * CAP
    fast = 8 if ntm % 8 == 0 else ntm
    hbm = pl.BlockSpec(memory_space=pltpu.HBM)
    vmem = pl.BlockSpec(memory_space=pltpu.VMEM)
    tiles = CAP * width // LANES
    latent_shape = jax.ShapeDtypeStruct((frames, half_rows, half_cols, width), BF16)
    dma = pltpu.SemaphoreType.DMA
    latent, arrived = pl.pallas_call(
        functools.partial(
            encode_kernel, ntm, nh, (frames, rows, cols, chans, width), (fast, ntm // fast)
        ),
        out_shape=(latent_shape, jax.ShapeDtypeStruct((owners, tiles, LANES), BF16)),
        in_specs=[hbm] * 9,
        out_specs=(hbm, hbm),
        scratch_shapes=[
            pltpu.VMEM((frames + 2, rows + 2, cols, chans), BF16),
            pltpu.VMEM((3, 3, chans, 2 * chans), BF16),
            pltpu.VMEM((3, 4, chans, 2 * chans), BF16),
            pltpu.VMEM((1, chans), F32),
            pltpu.VMEM((1, chans), F32),
            pltpu.VMEM(down_weight.shape, BF16),
            pltpu.VMEM(length_table.shape, F32),
            pltpu.VMEM(keep.shape, jnp.int32),
            pltpu.VMEM(keep.shape, jnp.int32),
            pltpu.VMEM(keep.shape, jnp.int32),
            pltpu.VMEM((frames, rows, cols, chans), F32),
            pltpu.VMEM((nh, frames, 16, chans), F32),
            pltpu.VMEM((2, frames * half_rows, LANES), F32),
            pltpu.VMEM((slots, toks), BF16),
            pltpu.VMEM((slots, width), F32),
            pltpu.VMEM((frames * half_rows, half_cols, width), BF16),
            pltpu.VMEM((owners, tiles, LANES), BF16),
            dma((12,)),
            dma((6,)),
            dma((6,)),
            dma((frames, nh - 1)),
            dma((frames, nh)),
            pltpu.SemaphoreType.REGULAR((3,)),
            dma((frames + 1,)),
            dma,
            dma,
        ],
        compiler_params=pltpu.CompilerParams(
            collective_id=0, has_side_effects=True, vmem_limit_bytes=48 * 1024 * 1024
        ),
        name="encode",
    )(
        video,
        conv_weight,
        norm_gain.reshape(1, chans),
        norm_bias.reshape(1, chans),
        down_weight,
        length_table,
        keep,
        run_length,
        owner,
    )
    routed, latent = pl.pallas_call(
        functools.partial(compact_kernel, owners, width),
        out_shape=(jax.ShapeDtypeStruct((slots, width), BF16), latent_shape),
        in_specs=[vmem, hbm],
        out_specs=(vmem, hbm),
        scratch_shapes=[dma],
        compiler_params=pltpu.CompilerParams(vmem_limit_bytes=48 * 1024 * 1024),
        name="compact",
    )(arrived, latent)
    return latent, routed


def solution(mesh):
    return jax.shard_map(
        functools.partial(on_device, mesh.shape["tm"], mesh.shape["height"]),
        mesh=mesh,
        in_specs=(
            P("tm", "height", None, None),
            P(),
            P(),
            P(),
            P(),
            P(),
            P("tm", "height", None),
            P("tm", "height", None),
            P("tm", "height", None),
        ),
        out_specs=(P("tm", "height", None, None), P(("tm", "height"), None)),
        check_vma=False,
    )
```

```python
import functools

import jax
import jax.numpy as jnp
from jax import lax
from jax.experimental import pallas as pl
from jax.experimental.pallas import tpu as pltpu
from jax.sharding import PartitionSpec as P

GROUPS = 32
LMAX = 8
CAP = 8
EPSILON = 1e-06
LANES = 128
EMPTY = 2.0**127
LIMIT = 2.0**126
MESH = pl.DeviceIdType.MESH
F32 = jnp.float32
BF16 = jnp.bfloat16


def dot(a, b):
    return jnp.dot(a, b, preferred_element_type=F32)


def dot_t(a, b, precision=None):
    return lax.dot_general(
        a, b, (((1,), (1,)), ((), ())), preferred_element_type=F32, precision=precision
    )


def iota(shape, dim):
    return lax.broadcasted_iota(jnp.int32, shape, dim)


def onehot(mask):
    return jnp.where(mask, 1.0, 0.0).astype(BF16)


def encode_kernel(
    ntm, nh, shapes, ways,
    video_in, weight_in, gain_in, bias_in, down_in, table_in, keep_in, run_in, owner_in,
    latent_out, arrived,
    xbuf, wpair, wlast, gain, bias, down, table, keep, run, owner,
    hidden, stat, codes, routes, extra, lat, pay,
    in_sem, halo_send, halo_recv, stat_send, stat_recv, ready, out_sem, go_sem, come_sem,
):
    frames, rows, cols, chans, width = shapes
    half_rows, half_cols = rows // 2, cols // 2
    patches = half_rows * half_cols
    toks = frames * patches
    owners = ntm * nh
    slots = owners * CAP
    me_t, me_h = lax.axis_index("tm"), lax.axis_index("height")
    me = me_t * nh + me_h
    next_t, last_t = lax.rem(me_t + 1, ntm), lax.rem(me_t + ntm - 1, ntm)
    up, down_h = lax.rem(me_h + nh - 1, nh), lax.rem(me_h + 1, nh)
    peers = [lax.rem(me_h + k, nh) for k in range(1, nh)]

    fast, slow = ways
    plane, line = me_t // fast, lax.rem(me_t, fast)
    rounds = [
        [(me_t, h) for h in peers],
        [(plane * fast + lax.rem(line + k, fast), me_h) for k in range(1, fast)],
        [(lax.rem(plane + k, slow) * fast + line, me_h) for k in range(1, slow)],
    ]
    sources = [(last_t, me_h)]
    sources += [target for group in rounds for target in group]
    barrier = pltpu.get_barrier_semaphore()
    for t, h in sources:
        pl.semaphore_signal(
            barrier, inc=1, device_id={"tm": t, "height": h}, device_id_type=MESH
        )

    loads = [
        (keep_in, keep), (run_in, run), (owner_in, owner), (table_in, table),
        (video_in, xbuf.at[pl.ds(2, frames), pl.ds(1, rows)]),
        (weight_in.at[:, :, 0], wpair.at[:, :, :, pl.ds(0, chans)]),
        (weight_in.at[:, :, 1], wpair.at[:, :, :, pl.ds(chans, chans)]),
        (weight_in.at[:, :, 2], wlast.at[:, pl.ds(0, 3), :, pl.ds(0, chans)]),
        (weight_in.at[:, :, 2], wlast.at[:, pl.ds(1, 3), :, pl.ds(chans, chans)]),
        (down_in, down), (gain_in, gain), (bias_in, bias),
    ]
    loads = [
        pltpu.make_async_copy(src, dst, in_sem.at[k]) for k, (src, dst) in enumerate(loads)
    ]
    for copy in loads:
        copy.start()
    wlast[:, 3, :, pl.ds(0, chans)] = jnp.zeros((3, chans, chans), BF16)
    wlast[:, 0, :, pl.ds(chans, chans)] = jnp.zeros((3, chans, chans), BF16)
    pl.semaphore_wait(barrier, len(sources))

    def halo(k, src, dst, t, h):
        return pltpu.make_async_remote_copy(
            src_ref=src, dst_ref=dst, send_sem=halo_send.at[k], recv_sem=halo_recv.at[k],
            device_id={"tm": t, "height": h}, device_id_type=MESH,
        )

    pair = pl.ds(frames - 2, 2)
    inner = pl.ds(1, rows - 2)
    to_up = halo(0, video_in.at[:, 0], xbuf.at[pl.ds(2, frames), rows + 1], me_t, up)
    to_down = halo(1, video_in.at[:, rows - 1], xbuf.at[pl.ds(2, frames), 0], me_t, down_h)
    top = halo(2, video_in.at[pair, 0], xbuf.at[pl.ds(0, 2), 1], next_t, me_h)
    bottom = halo(3, video_in.at[pair, rows - 1], xbuf.at[pl.ds(0, 2), rows], next_t, me_h)
    late = halo(4, video_in.at[frames - 1, inner], xbuf.at[1, pl.ds(2, rows - 2)], next_t, me_h)
    early = halo(5, video_in.at[frames - 2, inner], xbuf.at[0, pl.ds(2, rows - 2)], next_t, me_h)
    corner_up = halo(6, xbuf.at[pl.ds(0, 2), 1], xbuf.at[pl.ds(0, 2), rows + 1], me_t, up)
    corner_down = halo(7, xbuf.at[pl.ds(0, 2), rows], xbuf.at[pl.ds(0, 2), 0], me_t, down_h)
    halos = (top, bottom, to_up, to_down, late, early, corner_up, corner_down)
    for copy in halos[:6]:
        copy.start()

    def tell(k):
        for t, h in rounds[k]:
            pl.semaphore_signal(
                ready.at[k], inc=1, device_id={"tm": t, "height": h}, device_id_type=MESH
            )

    def hear(k):
        if rounds[k]:
            pl.semaphore_wait(ready.at[k], len(rounds[k]))

    tell(0)
    for copy in loads[:4]:
        copy.wait()
    codes[...] = jnp.zeros(codes.shape, F32)
    for t in range(frames):
        kept = keep[t] == 1
        where_to = jnp.where(kept, owner[t], owners)
        codes[0, pl.ds(t * half_rows, half_rows), pl.ds(0, half_cols)] = where_to.astype(F32)
        codes[1, pl.ds(t * half_rows, half_rows), pl.ds(0, half_cols)] = (
            run[t] - 1
        ).astype(F32)
    lines = frames * half_rows
    wide = codes.shape[2]
    spread_at = onehot(iota((wide, toks), 0) == lax.rem(iota((wide, toks), 1), half_cols))
    mine = iota((lines, toks), 0) == iota((lines, toks), 1) // half_cols
    code = jnp.sum(
        jnp.where(mine, dot(codes[0].astype(BF16), spread_at), 0.0), axis=0, keepdims=True
    )
    length = jnp.sum(
        jnp.where(mine, dot(codes[1].astype(BF16), spread_at), 0.0), axis=0, keepdims=True
    )
    code_i, length_i = code.astype(jnp.int32), length.astype(jnp.int32)
    member = iota((owners, toks), 0) == code_i
    before_lane = onehot(iota((LANES, LANES), 0) < iota((LANES, LANES), 1))
    carry = jnp.zeros((owners, 1), F32)
    for k in range(toks // LANES):
        at = slice(k * LANES, (k + 1) * LANES)
        block = jnp.where(member[:, at], 1.0, 0.0)
        ahead = dot(block.astype(BF16), before_lane) + carry
        carry = carry + jnp.sum(block, axis=1, keepdims=True)
        rank = jnp.sum(ahead * block, axis=0, keepdims=True).astype(jnp.int32)
        place = lax.rem(code_i[:, at] + (owners - me), owners)
        slot = jnp.where(code_i[:, at] < owners, place * CAP + rank, -1)
        routes[:, at] = onehot(iota((slots, LANES), 0) == slot)
    lanes_t = 4 * LMAX
    row_of = iota((lanes_t, toks), 0)
    which = onehot((lax.rem(row_of, LMAX) == length_i) | (row_of >= 3 * LMAX))
    part0 = table[...].astype(BF16)
    rest = table[...] - part0.astype(F32)
    part1 = rest.astype(BF16)
    part2 = (rest - part1.astype(F32)).astype(BF16)
    parts = jnp.concatenate(
        [part0.astype(F32), part1.astype(F32), part2.astype(F32), jnp.zeros((LMAX, width), F32)],
        axis=0,
    ).astype(BF16)
    picked = dot_t(routes[...], which)
    added = dot(picked.astype(BF16), parts)
    extra[...] = jnp.where(picked[:, 3 * LMAX : 3 * LMAX + 1] > 0.5, added, EMPTY)

    for copy in loads[4:]:
        copy.wait()
    hear(0)
    tell(1)
    top.wait_recv()
    corner_up.start()
    bottom.wait_recv()
    corner_down.start()

    first = iota((1, cols, chans), 1) == 0
    final = iota((1, cols, chans), 1) == cols - 1

    def gather(lines, a, b):
        return jnp.concatenate([xbuf[t + a, r + b] for t, r in lines], axis=0)

    def convolve(lines, paired, fresh):
        count = len(lines)
        window = jnp.concatenate(
            [gather(lines, a, b) for a in range(3) for b in range(3)], axis=1
        )
        taps = dot(window, wpair[...].reshape(9 * chans, 2 * chans))
        left = pltpu.roll(taps[:, :chans], 1, 0).reshape(count, cols, chans)
        out = taps[:, chans:].reshape(count, cols, chans) + jnp.where(first, 0.0, left)
        if paired:
            half = count // 2
            window = jnp.concatenate(
                [gather(lines[::2], a, b) for a in range(3) for b in range(4)], axis=1
            )
            taps = dot(window, wlast[...].reshape(12 * chans, 2 * chans))
            right = jnp.concatenate(
                [
                    pltpu.roll(
                        taps[:, k * chans : (k + 1) * chans], half * cols - 1, 0
                    ).reshape(half, 1, cols, chans)
                    for k in range(2)
                ],
                axis=1,
            )
        else:
            taps = dot(window, wlast[:, 0:3, :, 0:chans].reshape(9 * chans, chans))
            right = pltpu.roll(taps, count * cols - 1, 0)
        out = out + jnp.where(final, 0.0, right.reshape(count, cols, chans))
        for t in sorted({t for t, _ in lines}):
            mine = [k for k, line in enumerate(lines) if line[0] == t]
            for k in mine:
                hidden[t, lines[k][1]] = out[k]
            tiles = out[mine[0] : mine[-1] + 1].reshape(len(mine) * cols // 8, 8, chans)
            total, square = jnp.sum(tiles, axis=0), jnp.sum(tiles * tiles, axis=0)
            if not fresh:
                total = total + stat[me_h, t, pl.ds(0, 8)]
                square = square + stat[me_h, t, pl.ds(8, 8)]
            stat[me_h, t, pl.ds(0, 8)] = total
            stat[me_h, t, pl.ds(8, 8)] = square

    def clear_rows(at, count):
        @pl.when(me_h == 0)
        def _():
            xbuf[pl.ds(at, count), 0] = jnp.zeros((count, cols, chans), BF16)

        @pl.when(me_h == nh - 1)
        def _():
            xbuf[pl.ds(at, count), rows + 1] = jnp.zeros((count, cols, chans), BF16)

    def stat_copy(t, k):
        return pltpu.make_async_remote_copy(
            src_ref=stat.at[me_h, t], dst_ref=stat.at[me_h, t],
            send_sem=stat_send.at[t, k], recv_sem=stat_recv.at[t, me_h],
            device_id={"tm": me_t, "height": peers[k]}, device_id_type=MESH,
        )

    def stat_arrival(t, k):
        return pltpu.make_async_remote_copy(
            src_ref=stat.at[peers[k], t], dst_ref=stat.at[peers[k], t],
            send_sem=stat_send.at[t, k], recv_sem=stat_recv.at[t, peers[k]],
            device_id={"tm": me_t, "height": peers[k]}, device_id_type=MESH,
        )

    def send_stat(t):
        for k in range(nh - 1):
            stat_copy(t, k).start()

    group_of = chans // GROUPS
    same = jnp.where(
        iota((chans, chans), 0) // group_of == iota((chans, chans), 1) // group_of, 1.0, 0.0
    )
    count = rows * nh * cols * group_of

    def finish(t):
        for k in range(nh - 1):
            stat_arrival(t, k).wait_recv()
        summed = jnp.sum(stat[:, t], axis=0).reshape(2, 8, chans)
        summed = jnp.sum(summed, axis=1)
        pads = jnp.concatenate([summed, jnp.zeros((6, chans), F32)], axis=0)
        grouped = jnp.dot(
            pads, same, preferred_element_type=F32, precision=lax.Precision.HIGHEST
        ) / count
        average, squares = grouped[0:1], grouped[1:2]
        spread = squares - average * average
        scale = lax.rsqrt(spread + EPSILON) * gain[...]

        def act(r, b):
            h = hidden[t, r, pl.ds(b, half_cols, stride=2), :]
            v = 0.5 * ((h - average) * scale + bias[...])
            return (v * (1.0 + jnp.tanh(v))).astype(BF16)

        merged = jnp.concatenate(
            [
                jnp.concatenate(
                    [act(2 * i + a, b) for a in range(2) for b in range(2)], axis=1
                )
                for i in range(half_rows)
            ],
            axis=0,
        )
        lat[pl.ds(t * patches, patches)] = dot(merged, down[...]).astype(BF16)
        latent_copy(t).start()

    def latent_copy(t):
        return pltpu.make_async_copy(
            lat.at[pl.ds(t * patches, patches)], latent_out.at[t], out_sem.at[t]
        )

    for t in range(frames - 1, 1, -1):
        convolve([(t, r) for r in range(1, rows - 1)], True, True)
    to_up.wait_recv()
    to_down.wait_recv()
    clear_rows(2, frames)
    convolve([(t, r) for t in range(2, frames) for r in (0, rows - 1)], False, False)
    for t in range(frames - 1, 1, -1):
        send_stat(t)
    hear(1)
    tell(2)
    late.wait_recv()
    corner_up.wait_recv()
    corner_down.wait_recv()
    corner_up.wait_send()
    corner_down.wait_send()
    clear_rows(0, 2)

    @pl.when(me_t == 0)
    def _():
        xbuf[1] = jnp.zeros((rows + 2, cols, chans), BF16)

    convolve([(1, r) for r in range(rows)], True, True)
    send_stat(1)
    early.wait_recv()

    @pl.when(me_t == 0)
    def _():
        xbuf[0] = jnp.zeros((rows + 2, cols, chans), BF16)

    convolve([(0, r) for r in range(rows)], True, True)
    send_stat(0)
    hear(2)
    for t in range(frames - 1, 0, -1):
        finish(t)
    done = -(-patches // LANES) * LANES
    extra[...] += dot(routes[:, done:], lat[pl.ds(done, toks - done)])
    finish(0)
    batch = min(16, owners)

    def leave(i, _):
        at = pl.multiple_of(i * (batch * CAP), batch * CAP)
        here = pl.ds(at, batch * CAP)
        out = dot(routes[here, pl.ds(0, done)], lat[pl.ds(0, done)]) + extra[here]
        sides = [
            out[:, k * LANES : (k + 1) * LANES].reshape(batch, CAP, LANES)
            for k in range(width // LANES)
        ]
        pay[pl.ds(i * batch, batch)] = jnp.concatenate(sides, axis=1).astype(BF16)
        for j in range(batch):
            k = i * batch + j
            to = lax.rem(me + k, owners)

            def send():
                pltpu.make_async_remote_copy(
                    src_ref=pay.at[k], dst_ref=arrived.at[me],
                    send_sem=go_sem, recv_sem=come_sem,
                    device_id={"tm": to // nh, "height": lax.rem(to, nh)},
                    device_id_type=MESH,
                ).start()

            if j:
                send()
            else:
                pl.when(k > 0)(send)
        return 0

    lax.fori_loop(0, owners // batch, leave, 0)
    mine_copy = pltpu.make_async_copy(pay.at[0], arrived.at[me], out_sem.at[frames])
    mine_copy.start()
    for copy in halos[:6]:
        copy.wait_send()
    for t in range(frames):
        for k in range(nh - 1):
            stat_copy(t, k).wait_send()
        latent_copy(t).wait()
    mine_copy.wait()
    others = pl.ds(0, owners - 1)
    pltpu.make_async_copy(pay.at[others], arrived.at[others], come_sem).wait()
    pltpu.make_async_copy(pay.at[others], arrived.at[others], go_sem).wait()


def compact(arrived, owners, width):
    slots = owners * CAP
    block = min(LANES, slots)
    tall = arrived.astype(F32)
    sides = [
        tall[:, k * CAP : (k + 1) * CAP].reshape(slots, LANES) for k in range(width // LANES)
    ]
    rows = jnp.concatenate(sides, axis=1).astype(BF16)
    pick = onehot(iota((8, LANES), 1) == 0)
    lead = dot_t(pick, sides[0].astype(BF16))
    ahead_of = onehot(iota((block, block), 0) < iota((block, block), 1))
    carry = jnp.zeros((8, 1), F32)
    places = []
    for k in range(slots // block):
        valid = jnp.where(lead[:, k * block : (k + 1) * block] < LIMIT, 1.0, 0.0)
        place = dot(valid.astype(BF16), ahead_of) + carry
        carry = carry + jnp.sum(valid, axis=1, keepdims=True)
        places.append(jnp.where(valid > 0.5, place, -1.0)[0:1].astype(jnp.int32))
    chosen = jnp.concatenate(
        [onehot(iota((slots, block), 0) == place) for place in places], axis=1
    )
    return dot(chosen, rows).astype(BF16)


def compact_kernel(owners, width, arrived, latent_in, routed, latent_out, sem):
    copy = pltpu.make_async_copy(latent_in, latent_out, sem)
    copy.start()
    routed[...] = compact(arrived[...], owners, width)
    copy.wait()


def on_device(
    ntm, nh, video, conv_weight, norm_gain, norm_bias, down_weight, length_table, keep, run_length, owner
):
    frames, rows, cols, chans = video.shape
    width = down_weight.shape[1]
    half_rows, half_cols = rows // 2, cols // 2
    toks = frames * half_rows * half_cols
    owners = ntm * nh
    slots = owners * CAP
    fast = 8 if ntm % 8 == 0 else ntm
    hbm = pl.BlockSpec(memory_space=pltpu.HBM)
    vmem = pl.BlockSpec(memory_space=pltpu.VMEM)
    tiles = CAP * width // LANES
    latent_shape = jax.ShapeDtypeStruct((frames, half_rows * half_cols, width), BF16)
    dma = pltpu.SemaphoreType.DMA
    operands = (
        video,
        conv_weight,
        norm_gain.reshape(1, chans),
        norm_bias.reshape(1, chans),
        down_weight,
        length_table,
        keep,
        run_length,
        owner,
    )
    latent, arrived = pl.pallas_call(
        functools.partial(
            encode_kernel, ntm, nh, (frames, rows, cols, chans, width), (fast, ntm // fast)
        ),
        out_shape=(latent_shape, jax.ShapeDtypeStruct((owners, tiles, LANES), BF16)),
        in_specs=[hbm] * 9,
        out_specs=(hbm, hbm),
        scratch_shapes=[
            pltpu.VMEM((frames + 2, rows + 2, cols, chans), BF16),
            pltpu.VMEM((3, 3, chans, 2 * chans), BF16),
            pltpu.VMEM((3, 4, chans, 2 * chans), BF16),
            pltpu.VMEM((1, chans), F32),
            pltpu.VMEM((1, chans), F32),
            pltpu.VMEM(down_weight.shape, BF16),
            pltpu.VMEM(length_table.shape, F32),
            pltpu.VMEM(keep.shape, jnp.int32),
            pltpu.VMEM(keep.shape, jnp.int32),
            pltpu.VMEM(keep.shape, jnp.int32),
            pltpu.VMEM((frames, rows, cols, chans), F32),
            pltpu.VMEM((nh, frames, 16, chans), F32),
            pltpu.VMEM((2, frames * half_rows, LANES), F32),
            pltpu.VMEM((slots, toks), BF16),
            pltpu.VMEM((slots, width), F32),
            pltpu.VMEM((toks, width), BF16),
            pltpu.VMEM((owners, tiles, LANES), BF16),
            dma((12,)),
            dma((8,)),
            dma((8,)),
            dma((frames, nh - 1)),
            dma((frames, nh)),
            pltpu.SemaphoreType.REGULAR((3,)),
            dma((frames + 1,)),
            dma,
            dma,
        ],
        compiler_params=pltpu.CompilerParams(
            collective_id=0, has_side_effects=True, vmem_limit_bytes=48 * 1024 * 1024
        ),
        name="encode",
    )(*(pltpu.with_memory_space_constraint(array, pltpu.HBM) for array in operands))
    routed, latent = pl.pallas_call(
        functools.partial(compact_kernel, owners, width),
        out_shape=(jax.ShapeDtypeStruct((slots, width), BF16), latent_shape),
        in_specs=[vmem, hbm],
        out_specs=(vmem, hbm),
        scratch_shapes=[dma],
        compiler_params=pltpu.CompilerParams(vmem_limit_bytes=48 * 1024 * 1024),
        name="compact",
    )(arrived, latent)
    return latent.reshape(frames, half_rows, half_cols, width), routed


def solution(mesh):
    return jax.shard_map(
        functools.partial(on_device, mesh.shape["tm"], mesh.shape["height"]),
        mesh=mesh,
        in_specs=(
            P("tm", "height", None, None),
            P(),
            P(),
            P(),
            P(),
            P(),
            P("tm", "height", None),
            P("tm", "height", None),
            P("tm", "height", None),
        ),
        out_specs=(P("tm", "height", None, None), P(("tm", "height"), None)),
        check_vma=False,
    )
```

```python
import functools
import itertools

import jax
import jax.numpy as jnp
from jax import lax
from jax.experimental import pallas as pl
from jax.experimental.pallas import tpu as pltpu
from jax.sharding import PartitionSpec as P

GROUPS = 32
LMAX = 8
CAP = 8
EPSILON = 1e-06
LANES = 128
TURNS = ((3, 2, 1, 0), (2, 3, 1, 0), (2, 3, 1, 0), (1, 0))
EMPTY = 2.0**127
LIMIT = 2.0**126
MESH = pl.DeviceIdType.MESH
F32 = jnp.float32
BF16 = jnp.bfloat16


def dot(a, b):
    return jnp.dot(a, b, preferred_element_type=F32)


def dot_t(a, b, precision=None):
    return lax.dot_general(
        a, b, (((1,), (1,)), ((), ())), preferred_element_type=F32, precision=precision
    )


def iota(shape, dim):
    return lax.broadcasted_iota(jnp.int32, shape, dim)


def onehot(mask):
    return jnp.where(mask, 1.0, 0.0).astype(BF16)


def heights(patches, frames):
    head = (patches // LANES + 1) * LANES
    return head, head + -(-(frames - 1) * patches // LANES) * LANES


def encode_kernel(
    ntm, nh, shapes, ways,
    video_in, weight_in, gain_in, bias_in, down_in, table_in, keep_in, run_in, owner_in,
    latent_out, arrived,
    xbuf, wpair, wlast, gain, bias, down, table, keep, run, owner,
    hidden, stat, routes, extra, lat, total, pay,
    in_sem, halo_send, halo_recv, stat_send, stat_recv, ready, out_sem, go_sem, come_sem,
):
    frames, rows, cols, chans, width = shapes
    half_rows, half_cols = rows // 2, cols // 2
    patches = half_rows * half_cols
    toks = frames * patches
    owners = ntm * nh
    slots = owners * CAP
    head, taken = heights(patches, frames)
    me_t, me_h = lax.axis_index("tm"), lax.axis_index("height")
    me = me_t * nh + me_h
    next_t, last_t = lax.rem(me_t + 1, ntm), lax.rem(me_t + ntm - 1, ntm)
    up, down_h = lax.rem(me_h + nh - 1, nh), lax.rem(me_h + 1, nh)
    peers = [lax.rem(me_h + k, nh) for k in range(1, nh)]

    rows_x, planes = ways
    assert owners == 2 * nh * rows_x * planes and all(n & (n - 1) == 0 for n in (nh, *ways))

    even = lax.rem(me_t, 2) == 0
    has_next, has_last = me_t < ntm - 1, me_t > 0

    def signal(semaphore, t, h):
        pl.semaphore_signal(
            semaphore, inc=1, device_id={"tm": t, "height": h}, device_id_type=MESH
        )

    across = [
        [(me_t, h) for h in peers],
        [(me_t ^ (2 * k), me_h) for k in range(1, rows_x)],
        [(me_t ^ (2 * rows_x * k), me_h) for k in range(1, planes)],
    ]
    barrier = pltpu.get_barrier_semaphore()

    @pl.when(has_last)
    def _():
        signal(barrier, last_t, me_h)

    for t, h in across[0]:
        signal(barrier, t, h)

    @pl.when(even)
    def _():
        for t, h in across[1] + across[2]:
            signal(barrier, t, h)

    loads = [
        (keep_in, keep), (run_in, run), (owner_in, owner), (table_in, table),
        (video_in, xbuf.at[pl.ds(2, frames), pl.ds(1, rows)]),
        (weight_in.at[:, :, 0], wpair.at[:, :, :, pl.ds(0, chans)]),
        (weight_in.at[:, :, 1], wpair.at[:, :, :, pl.ds(chans, chans)]),
        (weight_in.at[:, :, 2], wlast.at[:, pl.ds(0, 3), :, pl.ds(0, chans)]),
        (weight_in.at[:, :, 2], wlast.at[:, pl.ds(1, 3), :, pl.ds(chans, chans)]),
        (down_in, down), (gain_in, gain), (bias_in, bias),
    ]
    loads = [
        pltpu.make_async_copy(src, dst, in_sem.at[k]) for k, (src, dst) in enumerate(loads)
    ]
    for copy in loads:
        copy.start()
    wlast[:, 3, :, pl.ds(0, chans)] = jnp.zeros((3, chans, chans), BF16)
    wlast[:, 0, :, pl.ds(chans, chans)] = jnp.zeros((3, chans, chans), BF16)
    awaited = nh - 1 + jnp.where(has_next, 1, 0)
    pl.semaphore_wait(barrier, awaited + jnp.where(even, rows_x + planes - 2, 0))

    def halo(k, src, dst, t, h):
        return pltpu.make_async_remote_copy(
            src_ref=src, dst_ref=dst, send_sem=halo_send.at[k], recv_sem=halo_recv.at[k],
            device_id={"tm": t, "height": h}, device_id_type=MESH,
        )

    pair = pl.ds(frames - 2, 2)
    inner = pl.ds(1, rows - 2)
    to_up = halo(0, video_in.at[:, 0], xbuf.at[pl.ds(2, frames), rows + 1], me_t, up)
    to_down = halo(1, video_in.at[:, rows - 1], xbuf.at[pl.ds(2, frames), 0], me_t, down_h)
    top = halo(2, video_in.at[pair, 0], xbuf.at[pl.ds(0, 2), 1], next_t, me_h)
    bottom = halo(3, video_in.at[pair, rows - 1], xbuf.at[pl.ds(0, 2), rows], next_t, me_h)
    late = halo(4, video_in.at[frames - 1, inner], xbuf.at[1, pl.ds(2, rows - 2)], next_t, me_h)
    early = halo(5, video_in.at[frames - 2, inner], xbuf.at[0, pl.ds(2, rows - 2)], next_t, me_h)
    corner_up = halo(6, xbuf.at[pl.ds(0, 2), 1], xbuf.at[pl.ds(0, 2), rows + 1], me_t, up)
    corner_down = halo(7, xbuf.at[pl.ds(0, 2), rows], xbuf.at[pl.ds(0, 2), 0], me_t, down_h)
    onward = (top, bottom, late, early)

    @pl.when(has_next)
    def _():
        for copy in onward[:2]:
            copy.start()

    to_up.start()
    to_down.start()

    @pl.when(has_next)
    def _():
        for copy in onward[2:]:
            copy.start()

    def tell(k):
        @pl.when(even)
        def _():
            for t, h in across[k] if k < 3 else [(next_t, me_h)]:
                signal(ready.at[k], t, h)

    def hear(k):
        if k == 3 or across[k]:

            @pl.when(even if k < 3 else jnp.logical_not(even))
            def _():
                pl.semaphore_wait(ready.at[k], len(across[k]) if k < 3 else 1)

    tell(0)
    for copy in loads[:4]:
        copy.wait()
    def along(pieces, filler):
        row = [pieces[r] for r in range(half_rows)]
        row += [jnp.full((1, head - patches), filler, jnp.int32)]
        row += [pieces[r] for r in range(half_rows, frames * half_rows)]
        row += [jnp.full((1, taken - head - (toks - patches)), filler, jnp.int32)]
        return jnp.concatenate([piece for piece in row if piece.shape[1]], axis=1)

    lines = [(t, slice(r, r + 1)) for t in range(frames) for r in range(half_rows)]
    place = []
    for t, r in lines:
        place.append(jnp.where(keep[t, r] == 1, owner[t, r] ^ me, -1))
    place = along(place, -1)
    length = along([run[t, r] - 1 for t, r in lines], -1)
    member = iota((owners, taken), 0) == place
    before_lane = onehot(iota((LANES, LANES), 0) < iota((LANES, LANES), 1))
    kept = jnp.zeros((owners, 1), F32)
    for k in range(taken // LANES):
        at = slice(k * LANES, (k + 1) * LANES)
        block = jnp.where(member[:, at], 1.0, 0.0)
        ahead = dot(block.astype(BF16), before_lane) + kept
        kept = kept + jnp.sum(block, axis=1, keepdims=True)
        rank = jnp.sum(ahead * block, axis=0, keepdims=True).astype(jnp.int32)
        slot = jnp.where(place[:, at] < 0, -1, place[:, at] * CAP + rank)
        chosen = iota((slots, LANES), 0) == slot
        if k == patches // LANES:
            partly = chosen
        else:
            routes[:, at] = onehot(chosen)
    at = slice(patches // LANES * LANES, (patches // LANES + 1) * LANES)
    unused = iota((owners, CAP, LANES), 1).astype(F32) >= kept.reshape(owners, 1, 1)
    mark = unused & (iota((owners, CAP, LANES), 2) == patches % LANES)
    routes[:, at] = jnp.maximum(
        onehot(partly).astype(F32), jnp.where(mark, 1.0, 0.0).reshape(slots, LANES)
    ).astype(BF16)
    lat[pl.ds(patches, head - patches)] = jnp.where(
        iota((head - patches, width), 0) == 0, EMPTY, 0.0
    ).astype(BF16)
    if taken > head + toks - patches:
        tail = taken - head - (toks - patches)
        lat[pl.ds(taken - tail, tail)] = jnp.zeros((tail, width), BF16)
    row_of = iota((4 * LMAX, taken), 0)
    which = (lax.rem(row_of, LMAX) == length) & (row_of < 3 * LMAX)
    which = jnp.where(which, 1.0, 0.0).T.astype(BF16)
    part0 = table[...].astype(BF16)
    rest = table[...] - part0.astype(F32)
    part1 = rest.astype(BF16)
    part2 = (rest - part1.astype(F32)).astype(BF16)
    parts = jnp.concatenate(
        [part0.astype(F32), part1.astype(F32), part2.astype(F32), jnp.zeros((LMAX, width), F32)],
        axis=0,
    ).astype(BF16)
    extra[...] = dot(which, parts)

    for copy in loads[4:]:
        copy.wait()
    hear(0)
    tell(1)

    first = iota((1, 8, chans), 1) == 0
    final = iota((1, 8, chans), 1) == 7

    def gather(lines, a, b):
        return jnp.concatenate([xbuf[t + a, r + b] for t, r in lines], axis=0)

    def convolve(lines, paired, afters=(0, 1, 2)):
        count = len(lines)
        window = jnp.concatenate(
            [gather(lines, a, b) for a in afters for b in range(3)], axis=1
        )
        used = slice(afters[0], afters[-1] + 1)
        taps = dot(window, wpair[used].reshape(-1, 2 * chans))
        left = pltpu.roll(taps[:, :chans], 1, 0).reshape(count, cols, chans)
        left = jnp.concatenate([jnp.where(first, 0.0, left[:, :8]), left[:, 8:]], axis=1)
        out = taps[:, chans:].reshape(count, cols, chans) + left
        if paired:
            half = count // 2
            window = jnp.concatenate(
                [gather(lines[::2], a, b) for a in afters for b in range(4)], axis=1
            )
            taps = dot(window, wlast[used].reshape(-1, 2 * chans))
            right = jnp.concatenate(
                [
                    pltpu.roll(
                        taps[:, k * chans : (k + 1) * chans], half * cols - 1, 0
                    ).reshape(half, 1, cols, chans)
                    for k in range(2)
                ],
                axis=1,
            )
        else:
            taps = dot(window, wlast[used, 0:3, :, 0:chans].reshape(-1, chans))
            right = pltpu.roll(taps, count * cols - 1, 0)
        right = right.reshape(count, cols, chans)
        out = out + jnp.concatenate(
            [right[:, :-8], jnp.where(final, 0.0, right[:, -8:])], axis=1
        )
        for t in sorted({t for t, _ in lines}):
            mine = [k for k, line in enumerate(lines) if line[0] == t]
            if afters == (0,):
                out = out + hidden[t]
            for k in mine:
                hidden[t, lines[k][1]] = out[k]
            if afters == (1, 2):
                continue
            tiles = out[mine[0] : mine[-1] + 1].reshape(len(mine) * cols // 8, 8, chans)
            total, square = jnp.sum(tiles, axis=0), jnp.sum(tiles * tiles, axis=0)
            if not paired:
                total = total + stat[me_h, t, pl.ds(0, 8)]
                square = square + stat[me_h, t, pl.ds(8, 8)]
            stat[me_h, t, pl.ds(0, 8)] = total
            stat[me_h, t, pl.ds(8, 8)] = square

    def clear_rows(at, count):
        @pl.when(me_h == 0)
        def _():
            xbuf[pl.ds(at, count), 0] = jnp.zeros((count, cols, chans), BF16)

        @pl.when(me_h == nh - 1)
        def _():
            xbuf[pl.ds(at, count), rows + 1] = jnp.zeros((count, cols, chans), BF16)

    def stat_copy(t, k):
        return pltpu.make_async_remote_copy(
            src_ref=stat.at[me_h, t], dst_ref=stat.at[me_h, t],
            send_sem=stat_send.at[t, k], recv_sem=stat_recv.at[t, me_h],
            device_id={"tm": me_t, "height": peers[k]}, device_id_type=MESH,
        )

    def stat_arrival(t, k):
        return pltpu.make_async_remote_copy(
            src_ref=stat.at[peers[k], t], dst_ref=stat.at[peers[k], t],
            send_sem=stat_send.at[t, k], recv_sem=stat_recv.at[t, peers[k]],
            device_id={"tm": me_t, "height": peers[k]}, device_id_type=MESH,
        )

    def send_stat(t):
        for k in range(nh - 1):
            stat_copy(t, k).start()

    group_of = chans // GROUPS
    same = onehot(iota((chans, chans), 0) // group_of == iota((chans, chans), 1) // group_of)
    count = rows * nh * cols * group_of

    def finish(times):
        for t in times:
            for k in range(nh - 1):
                stat_arrival(t, k).wait_recv()
        sums = [
            jnp.sum(jnp.sum(stat[:, t], axis=0).reshape(2, 8, chans), axis=1) for t in times
        ]
        sums = jnp.concatenate(sums + [jnp.zeros((8 - 2 * len(times), chans), F32)], axis=0)
        part0 = sums.astype(BF16).astype(F32)
        part1 = (sums - part0).astype(BF16).astype(F32)
        parts = jnp.concatenate([part0, part1, sums - part0 - part1], axis=0).astype(BF16)
        grouped = dot(parts, same)
        grouped = (grouped[0:8] + grouped[8:16] + grouped[16:24]) / count
        for k, t in enumerate(times):
            average, squares = grouped[2 * k : 2 * k + 1], grouped[2 * k + 1 : 2 * k + 2]
            spread = squares - average * average
            finish_frame(t, average, 0.5 * (lax.rsqrt(spread + EPSILON) * gain[...]))

    def finish_frame(t, average, scale):
        shift = 0.5 * bias[...]

        def act(r, b):
            h = hidden[t, r, pl.ds(b, half_cols, stride=2), :]
            v = (h - average) * scale + shift
            return (v + v * jnp.tanh(v)).astype(BF16)

        merged = jnp.concatenate(
            [
                jnp.concatenate(
                    [act(2 * i + a, b) for a in range(2) for b in range(2)], axis=1
                )
                for i in range(half_rows)
            ],
            axis=0,
        )
        latent = dot(merged, down[...]).astype(BF16)
        latent_out[t] = latent
        at = pl.ds(0 if t == 0 else head + (t - 1) * patches, patches)
        lat[at] = (latent.astype(F32) + extra[at]).astype(BF16)

    interior, edges = range(1, rows - 1), (0, rows - 1)
    for t in range(frames - 1, 1, -1):
        convolve([(t, r) for r in interior], True)

    @pl.when(has_last)
    def _():
        top.wait_recv()
        corner_up.start()
        bottom.wait_recv()
        corner_down.start()

    hear(1)
    tell(2)
    to_up.wait_recv()
    to_down.wait_recv()
    clear_rows(2, frames)
    convolve([(t, r) for t in range(2, frames) for r in edges], False)
    for t in range(frames - 1, 1, -1):
        send_stat(t)

    @pl.when(has_last)
    def _():
        late.wait_recv()

    @pl.when(jnp.logical_not(has_last))
    def _():
        xbuf[0:2] = jnp.zeros((2, rows + 2, cols, chans), BF16)

    convolve([(1, r) for r in interior], True)
    convolve([(0, r) for r in interior], True, (1, 2))

    @pl.when(has_last)
    def _():
        corner_up.wait_recv()
        corner_down.wait_recv()

    clear_rows(0, 2)
    convolve([(1, r) for r in edges], False)
    send_stat(1)
    convolve([(0, r) for r in edges], False, (1, 2))

    @pl.when(has_last)
    def _():
        early.wait_recv()

    convolve([(0, r) for r in range(rows)], True, (0,))
    send_stat(0)
    hear(2)
    tell(3)
    finish(range(frames - 1, 0, -1))
    rest = pl.ds(head, taken - head)
    total[...] = dot(routes[:, rest], lat[rest])
    finish([0])
    hear(3)
    batch = owners // planes
    turns = [[k for k in order if k < n] for order, n in zip(TURNS, (planes, rows_x, nh, 2))]
    for z in turns[0]:
        here = pl.ds(z * batch * CAP, batch * CAP)
        out = dot(routes[here, pl.ds(0, head)], lat[pl.ds(0, head)]) + total[here]
        sides = [
            out[:, k * LANES : (k + 1) * LANES].reshape(batch, CAP, LANES)
            for k in range(width // LANES)
        ]
        pay[pl.ds(z * batch, batch)] = jnp.concatenate(sides, axis=1).astype(BF16)
        for x, h, core in itertools.product(*turns[1:]):
            t = (z * rows_x + x) * 2 + core
            k = t * nh + h
            if k:
                pltpu.make_async_remote_copy(
                    src_ref=pay.at[k], dst_ref=arrived.at[me],
                    send_sem=go_sem, recv_sem=come_sem,
                    device_id={"tm": me_t ^ t, "height": me_h ^ h}, device_id_type=MESH,
                ).start()
    mine_copy = pltpu.make_async_copy(pay.at[0], arrived.at[me], out_sem)
    mine_copy.start()

    @pl.when(has_next)
    def _():
        for copy in onward:
            copy.wait_send()

    @pl.when(has_last)
    def _():
        corner_up.wait_send()
        corner_down.wait_send()

    to_up.wait_send()
    to_down.wait_send()
    for t in range(frames):
        for k in range(nh - 1):
            stat_copy(t, k).wait_send()
    mine_copy.wait()
    others = pl.ds(0, owners - 1)
    pltpu.make_async_copy(pay.at[others], arrived.at[others], come_sem).wait()
    pltpu.make_async_copy(pay.at[others], arrived.at[others], go_sem).wait()


def compact(arrived, owners, width):
    slots = owners * CAP
    block = min(LANES, slots)
    tall = arrived.astype(F32)
    sides = [
        tall[:, k * CAP : (k + 1) * CAP].reshape(slots, LANES) for k in range(width // LANES)
    ]
    rows = jnp.concatenate(sides, axis=1).astype(BF16)
    pick = onehot(iota((8, LANES), 1) == 0)
    lead = dot_t(pick, sides[0].astype(BF16))
    ahead_of = onehot(iota((block, block), 0) < iota((block, block), 1))
    carry = jnp.zeros((8, 1), F32)
    places = []
    for k in range(slots // block):
        valid = jnp.where(lead[:, k * block : (k + 1) * block] < LIMIT, 1.0, 0.0)
        place = dot(valid.astype(BF16), ahead_of) + carry
        carry = carry + jnp.sum(valid, axis=1, keepdims=True)
        places.append(jnp.where(valid > 0.5, place, -1.0)[0:1].astype(jnp.int32))
    chosen = jnp.concatenate(
        [onehot(iota((slots, block), 0) == place) for place in places], axis=1
    )
    return dot(chosen, rows).astype(BF16)


def compact_kernel(owners, width, arrived, latent_in, routed, latent_out, sem):
    copy = pltpu.make_async_copy(latent_in, latent_out, sem)
    copy.start()
    routed[...] = compact(arrived[...], owners, width)
    copy.wait()


def on_device(
    ntm, nh, video, conv_weight, norm_gain, norm_bias, down_weight, length_table, keep, run_length, owner
):
    frames, rows, cols, chans = video.shape
    width = down_weight.shape[1]
    half_rows, half_cols = rows // 2, cols // 2
    toks = frames * half_rows * half_cols
    owners = ntm * nh
    slots = owners * CAP
    _, taken = heights(half_rows * half_cols, frames)
    ways = (4, 4) if ntm == 32 else (ntm // 2, 1)
    hbm = pl.BlockSpec(memory_space=pltpu.HBM)
    vmem = pl.BlockSpec(memory_space=pltpu.VMEM)
    tiles = CAP * width // LANES
    latent_shape = jax.ShapeDtypeStruct((frames, half_rows * half_cols, width), BF16)
    dma = pltpu.SemaphoreType.DMA
    operands = (
        video,
        conv_weight,
        norm_gain.reshape(1, chans),
        norm_bias.reshape(1, chans),
        down_weight,
        length_table,
        keep,
        run_length,
        owner,
    )
    latent, arrived = pl.pallas_call(
        functools.partial(
            encode_kernel, ntm, nh, (frames, rows, cols, chans, width), ways
        ),
        out_shape=(latent_shape, jax.ShapeDtypeStruct((owners, tiles, LANES), BF16)),
        in_specs=[hbm] * 9,
        out_specs=(vmem, vmem),
        scratch_shapes=[
            pltpu.VMEM((frames + 2, rows + 2, cols, chans), BF16),
            pltpu.VMEM((3, 3, chans, 2 * chans), BF16),
            pltpu.VMEM((3, 4, chans, 2 * chans), BF16),
            pltpu.VMEM((1, chans), F32),
            pltpu.VMEM((1, chans), F32),
            pltpu.VMEM(down_weight.shape, BF16),
            pltpu.VMEM(length_table.shape, F32),
            pltpu.VMEM(keep.shape, jnp.int32),
            pltpu.VMEM(keep.shape, jnp.int32),
            pltpu.VMEM(keep.shape, jnp.int32),
            pltpu.VMEM((frames, rows, cols, chans), F32),
            pltpu.VMEM((nh, frames, 16, chans), F32),
            pltpu.VMEM((slots, taken), BF16),
            pltpu.VMEM((taken, width), F32),
            pltpu.VMEM((taken, width), BF16),
            pltpu.VMEM((slots, width), F32),
            pltpu.VMEM((owners, tiles, LANES), BF16),
            dma((12,)),
            dma((8,)),
            dma((8,)),
            dma((frames, nh - 1)),
            dma((frames, nh)),
            pltpu.SemaphoreType.REGULAR((4,)),
            dma,
            dma,
            dma,
        ],
        compiler_params=pltpu.CompilerParams(
            collective_id=0, has_side_effects=True, vmem_limit_bytes=48 * 1024 * 1024
        ),
        name="encode",
    )(*(pltpu.with_memory_space_constraint(array, pltpu.HBM) for array in operands))
    routed, latent = pl.pallas_call(
        functools.partial(compact_kernel, owners, width),
        out_shape=(jax.ShapeDtypeStruct((slots, width), BF16), latent_shape),
        in_specs=[vmem, hbm],
        out_specs=(vmem, hbm),
        scratch_shapes=[dma],
        compiler_params=pltpu.CompilerParams(vmem_limit_bytes=48 * 1024 * 1024),
        name="compact",
    )(arrived, latent)
    return latent.reshape(frames, half_rows, half_cols, width), routed


def solution(mesh):
    return jax.shard_map(
        functools.partial(on_device, mesh.shape["tm"], mesh.shape["height"]),
        mesh=mesh,
        in_specs=(
            P("tm", "height", None, None),
            P(),
            P(),
            P(),
            P(),
            P(),
            P("tm", "height", None),
            P("tm", "height", None),
            P("tm", "height", None),
        ),
        out_specs=(P("tm", "height", None, None), P(("tm", "height"), None)),
        check_vma=False,
    )
```

```python
import functools
import itertools

import jax
import jax.numpy as jnp
from jax import lax
from jax.experimental import pallas as pl
from jax.experimental.pallas import tpu as pltpu
from jax.sharding import PartitionSpec as P

GROUPS = 32
LMAX = 8
CAP = 8
EPSILON = 1e-06
LANES = 128
TURNS = ((2, 3, 1, 0), (2, 3, 1, 0), (1, 0))
EMPTY = 2.0**127
LIMIT = 2.0**126
MESH = pl.DeviceIdType.MESH
F32 = jnp.float32
BF16 = jnp.bfloat16


def dot(a, b):
    return jnp.dot(a, b, preferred_element_type=F32)


def dot_t(a, b, precision=None):
    return lax.dot_general(
        a, b, (((1,), (1,)), ((), ())), preferred_element_type=F32, precision=precision
    )


def iota(shape, dim):
    return lax.broadcasted_iota(jnp.int32, shape, dim)


def onehot(mask):
    return jnp.where(mask, 1.0, 0.0).astype(BF16)


def heights(patches, frames):
    head = (patches // LANES + 1) * LANES
    return head, head + -(-(frames - 1) * patches // LANES) * LANES


def encode_kernel(
    ntm, nh, shapes, ways,
    video_in, weight_in, gain_in, bias_in, down_in, table_in, keep_in, run_in, owner_in,
    latent_out, arrived,
    xbuf, wpair, wlast, gain, bias, down, table, keep, run, owner,
    hidden, stat, routes, extra, lat, total, pay,
    in_sem, halo_send, halo_recv, stat_send, stat_recv, ready, out_sem, go_sem, come_sem,
):
    frames, rows, cols, chans, width = shapes
    half_rows, half_cols = rows // 2, cols // 2
    patches = half_rows * half_cols
    toks = frames * patches
    owners = ntm * nh
    slots = owners * CAP
    head, taken = heights(patches, frames)
    me_t, me_h = lax.axis_index("tm"), lax.axis_index("height")
    me = me_t * nh + me_h
    next_t, last_t = lax.rem(me_t + 1, ntm), lax.rem(me_t + ntm - 1, ntm)
    up, down_h = lax.rem(me_h + nh - 1, nh), lax.rem(me_h + 1, nh)
    peers = [lax.rem(me_h + k, nh) for k in range(1, nh)]

    rows_x, planes = ways
    assert owners == 2 * nh * rows_x * planes and all(n & (n - 1) == 0 for n in (nh, *ways))

    even = lax.rem(me_t, 2) == 0
    has_next, has_last = me_t < ntm - 1, me_t > 0

    def signal(semaphore, t, h):
        pl.semaphore_signal(
            semaphore, inc=1, device_id={"tm": t, "height": h}, device_id_type=MESH
        )

    at_x, at_z = lax.rem(me_t // 2, rows_x), me_t // (2 * rows_x)
    first_x = even & (at_x == 0)
    first_z = first_x & (at_z == 0)
    later_x, later_z = even & (at_x > 0), first_x & (at_z > 0)
    to_first_x, to_first_z = me_t - 2 * at_x, 0
    all_x = [me_t + 2 * k for k in range(1, rows_x)]
    all_z = [2 * rows_x * k for k in range(1, planes)]
    relay = [
        (even, [(me_t, h) for h in peers], even, nh - 1),
        (later_x, [(to_first_x, me_h)], first_x, rows_x - 1),
        (later_z, [(to_first_z, me_h)], first_z, planes - 1),
        (first_z, [(t, me_h) for t in all_z], later_z, 1),
        (first_x, [(me_t + k, me_h) for k in range(1, 2 * rows_x)], jnp.logical_not(first_x), 1),
    ]
    barrier = pltpu.get_barrier_semaphore()

    @pl.when(has_last)
    def _():
        signal(barrier, last_t, me_h)

    for h in peers:
        signal(barrier, me_t, h)

    @pl.when(first_x)
    def _():
        for t in all_x:
            signal(barrier, t, me_h)

    @pl.when(first_z)
    def _():
        for t in all_z:
            signal(barrier, t, me_h)

    loads = [
        (keep_in, keep), (run_in, run), (owner_in, owner), (table_in, table),
        (video_in, xbuf.at[pl.ds(2, frames), pl.ds(1, rows)]),
        (weight_in.at[:, :, 0], wpair.at[:, :, :, pl.ds(0, chans)]),
        (weight_in.at[:, :, 1], wpair.at[:, :, :, pl.ds(chans, chans)]),
        (weight_in.at[:, :, 2], wlast.at[:, pl.ds(0, 3), :, pl.ds(0, chans)]),
        (weight_in.at[:, :, 2], wlast.at[:, pl.ds(1, 3), :, pl.ds(chans, chans)]),
        (down_in, down), (gain_in, gain), (bias_in, bias),
    ]
    loads = [
        pltpu.make_async_copy(src, dst, in_sem.at[k]) for k, (src, dst) in enumerate(loads)
    ]
    for copy in loads:
        copy.start()
    wlast[:, 3, :, pl.ds(0, chans)] = jnp.zeros((3, chans, chans), BF16)
    wlast[:, 0, :, pl.ds(chans, chans)] = jnp.zeros((3, chans, chans), BF16)
    awaited = nh - 1 + jnp.where(has_next, 1, 0)
    pl.semaphore_wait(barrier, awaited + jnp.where(later_x | later_z, 1, 0))

    def halo(k, src, dst, t, h):
        return pltpu.make_async_remote_copy(
            src_ref=src, dst_ref=dst, send_sem=halo_send.at[k], recv_sem=halo_recv.at[k],
            device_id={"tm": t, "height": h}, device_id_type=MESH,
        )

    pair = pl.ds(frames - 2, 2)
    inner = pl.ds(1, rows - 2)
    to_up = halo(0, video_in.at[:, 0], xbuf.at[pl.ds(2, frames), rows + 1], me_t, up)
    to_down = halo(1, video_in.at[:, rows - 1], xbuf.at[pl.ds(2, frames), 0], me_t, down_h)
    top = halo(2, video_in.at[pair, 0], xbuf.at[pl.ds(0, 2), 1], next_t, me_h)
    bottom = halo(3, video_in.at[pair, rows - 1], xbuf.at[pl.ds(0, 2), rows], next_t, me_h)
    late = halo(4, video_in.at[frames - 1, inner], xbuf.at[1, pl.ds(2, rows - 2)], next_t, me_h)
    early = halo(5, video_in.at[frames - 2, inner], xbuf.at[0, pl.ds(2, rows - 2)], next_t, me_h)
    corner_up = halo(6, xbuf.at[pl.ds(0, 2), 1], xbuf.at[pl.ds(0, 2), rows + 1], me_t, up)
    corner_down = halo(7, xbuf.at[pl.ds(0, 2), rows], xbuf.at[pl.ds(0, 2), 0], me_t, down_h)
    onward = (top, bottom, late, early)

    @pl.when(has_next)
    def _():
        for copy in onward[:2]:
            copy.start()

    to_up.start()
    to_down.start()

    @pl.when(has_next)
    def _():
        for copy in onward[2:]:
            copy.start()

    def tell(k):
        if k in (0, 4) or (rows_x, planes)[k in (2, 3)] > 1:

            @pl.when(relay[k][0])
            def _():
                for t, h in relay[k][1]:
                    signal(ready.at[k], t, h)

    def hear(k):
        if k in (0, 4) or (rows_x, planes)[k in (2, 3)] > 1:

            @pl.when(relay[k][2])
            def _():
                pl.semaphore_wait(ready.at[k], relay[k][3])

    tell(0)
    for copy in loads[:4]:
        copy.wait()
    def along(pieces, filler):
        row = [pieces[r] for r in range(half_rows)]
        row += [jnp.full((1, head - patches), filler, jnp.int32)]
        row += [pieces[r] for r in range(half_rows, frames * half_rows)]
        row += [jnp.full((1, taken - head - (toks - patches)), filler, jnp.int32)]
        return jnp.concatenate([piece for piece in row if piece.shape[1]], axis=1)

    lines = [(t, slice(r, r + 1)) for t in range(frames) for r in range(half_rows)]
    place = []
    for t, r in lines:
        place.append(jnp.where(keep[t, r] == 1, owner[t, r] ^ me, -1))
    place = along(place, -1)
    length = along([run[t, r] - 1 for t, r in lines], -1)
    member = iota((owners, taken), 0) == place
    before_lane = onehot(iota((LANES, LANES), 0) < iota((LANES, LANES), 1))
    kept = jnp.zeros((owners, 1), F32)
    for k in range(taken // LANES):
        at = slice(k * LANES, (k + 1) * LANES)
        block = jnp.where(member[:, at], 1.0, 0.0)
        ahead = dot(block.astype(BF16), before_lane) + kept
        kept = kept + jnp.sum(block, axis=1, keepdims=True)
        rank = jnp.sum(ahead * block, axis=0, keepdims=True).astype(jnp.int32)
        slot = jnp.where(place[:, at] < 0, -1, place[:, at] * CAP + rank)
        chosen = iota((slots, LANES), 0) == slot
        if k == patches // LANES:
            partly = chosen
        else:
            routes[:, at] = onehot(chosen)
    at = slice(patches // LANES * LANES, (patches // LANES + 1) * LANES)
    unused = iota((owners, CAP, LANES), 1).astype(F32) >= kept.reshape(owners, 1, 1)
    mark = unused & (iota((owners, CAP, LANES), 2) == patches % LANES)
    routes[:, at] = jnp.maximum(
        onehot(partly).astype(F32), jnp.where(mark, 1.0, 0.0).reshape(slots, LANES)
    ).astype(BF16)
    lat[pl.ds(patches, head - patches)] = jnp.where(
        iota((head - patches, width), 0) == 0, EMPTY, 0.0
    ).astype(BF16)
    if taken > head + toks - patches:
        tail = taken - head - (toks - patches)
        lat[pl.ds(taken - tail, tail)] = jnp.zeros((tail, width), BF16)
    row_of = iota((4 * LMAX, taken), 0)
    which = (lax.rem(row_of, LMAX) == length) & (row_of < 3 * LMAX)
    which = jnp.where(which, 1.0, 0.0).T.astype(BF16)
    part0 = table[...].astype(BF16)
    rest = table[...] - part0.astype(F32)
    part1 = rest.astype(BF16)
    part2 = (rest - part1.astype(F32)).astype(BF16)
    parts = jnp.concatenate(
        [part0.astype(F32), part1.astype(F32), part2.astype(F32), jnp.zeros((LMAX, width), F32)],
        axis=0,
    ).astype(BF16)
    extra[...] = dot(which, parts)

    for copy in loads[4:]:
        copy.wait()
    hear(0)
    tell(1)

    first = iota((1, 8, chans), 1) == 0
    final = iota((1, 8, chans), 1) == 7

    def gather(lines, a, b):
        return jnp.concatenate([xbuf[t + a, r + b] for t, r in lines], axis=0)

    def convolve(lines, paired, afters=(0, 1, 2), more=False, sums=True):
        count = len(lines)
        window = jnp.concatenate(
            [gather(lines, a, b) for a in afters for b in range(3)], axis=1
        )
        used = slice(afters[0], afters[-1] + 1)
        taps = dot(window, wpair[used].reshape(-1, 2 * chans))
        left = pltpu.roll(taps[:, :chans], 1, 0).reshape(count, cols, chans)
        left = jnp.concatenate([jnp.where(first, 0.0, left[:, :8]), left[:, 8:]], axis=1)
        out = taps[:, chans:].reshape(count, cols, chans) + left
        if paired:
            half = count // 2
            window = jnp.concatenate(
                [gather(lines[::2], a, b) for a in afters for b in range(4)], axis=1
            )
            taps = dot(window, wlast[used].reshape(-1, 2 * chans))
            right = jnp.concatenate(
                [
                    pltpu.roll(
                        taps[:, k * chans : (k + 1) * chans], half * cols - 1, 0
                    ).reshape(half, 1, cols, chans)
                    for k in range(2)
                ],
                axis=1,
            )
        else:
            taps = dot(window, wlast[used, 0:3, :, 0:chans].reshape(-1, chans))
            right = pltpu.roll(taps, count * cols - 1, 0)
        right = right.reshape(count, cols, chans)
        out = out + jnp.concatenate(
            [right[:, :-8], jnp.where(final, 0.0, right[:, -8:])], axis=1
        )
        for t in sorted({t for t, _ in lines}):
            mine = [k for k, line in enumerate(lines) if line[0] == t]
            part = out[mine[0] : mine[-1] + 1]
            if more:
                part = part + hidden[t, pl.ds(lines[mine[0]][1], len(mine))]
            for k in mine:
                hidden[t, lines[k][1]] = part[k - mine[0]]
            if not sums:
                continue
            tiles = part.reshape(len(mine) * cols // 8, 8, chans)
            total, square = jnp.sum(tiles, axis=0), jnp.sum(tiles * tiles, axis=0)
            if not paired:
                total = total + stat[me_h, t, pl.ds(0, 8)]
                square = square + stat[me_h, t, pl.ds(8, 8)]
            stat[me_h, t, pl.ds(0, 8)] = total
            stat[me_h, t, pl.ds(8, 8)] = square

    def clear_rows(at, count):
        @pl.when(me_h == 0)
        def _():
            xbuf[pl.ds(at, count), 0] = jnp.zeros((count, cols, chans), BF16)

        @pl.when(me_h == nh - 1)
        def _():
            xbuf[pl.ds(at, count), rows + 1] = jnp.zeros((count, cols, chans), BF16)

    def stat_copy(t, k):
        return pltpu.make_async_remote_copy(
            src_ref=stat.at[me_h, t], dst_ref=stat.at[me_h, t],
            send_sem=stat_send.at[t, k], recv_sem=stat_recv.at[t, me_h],
            device_id={"tm": me_t, "height": peers[k]}, device_id_type=MESH,
        )

    def stat_arrival(t, k):
        return pltpu.make_async_remote_copy(
            src_ref=stat.at[peers[k], t], dst_ref=stat.at[peers[k], t],
            send_sem=stat_send.at[t, k], recv_sem=stat_recv.at[t, peers[k]],
            device_id={"tm": me_t, "height": peers[k]}, device_id_type=MESH,
        )

    def send_stat(t):
        for k in range(nh - 1):
            stat_copy(t, k).start()

    group_of = chans // GROUPS
    same = onehot(iota((chans, chans), 0) // group_of == iota((chans, chans), 1) // group_of)
    count = rows * nh * cols * group_of

    def finish(times):
        for t in times:
            for k in range(nh - 1):
                stat_arrival(t, k).wait_recv()
        sums = [
            jnp.sum(jnp.sum(stat[:, t], axis=0).reshape(2, 8, chans), axis=1) for t in times
        ]
        sums = jnp.concatenate(sums + [jnp.zeros((8 - 2 * len(times), chans), F32)], axis=0)
        part0 = sums.astype(BF16).astype(F32)
        part1 = (sums - part0).astype(BF16).astype(F32)
        parts = jnp.concatenate([part0, part1, sums - part0 - part1], axis=0).astype(BF16)
        grouped = dot(parts, same)
        grouped = (grouped[0:8] + grouped[8:16] + grouped[16:24]) / count
        for k, t in enumerate(times):
            average, squares = grouped[2 * k : 2 * k + 1], grouped[2 * k + 1 : 2 * k + 2]
            spread = squares - average * average
            finish_frame(t, average, 0.5 * (lax.rsqrt(spread + EPSILON) * gain[...]))

    def finish_frame(t, average, scale):
        shift = 0.5 * bias[...]

        def act(r, b):
            h = hidden[t, r, pl.ds(b, half_cols, stride=2), :]
            v = (h - average) * scale + shift
            return (v + v * jnp.tanh(v)).astype(BF16)

        merged = jnp.concatenate(
            [
                jnp.concatenate(
                    [act(2 * i + a, b) for a in range(2) for b in range(2)], axis=1
                )
                for i in range(half_rows)
            ],
            axis=0,
        )
        latent = dot(merged, down[...]).astype(BF16)
        latent_out[t] = latent
        at = pl.ds(0 if t == 0 else head + (t - 1) * patches, patches)
        lat[at] = (latent.astype(F32) + extra[at]).astype(BF16)

    interior, edges = range(1, rows - 1), (0, rows - 1)
    for t in range(frames - 1, 1, -1):
        convolve([(t, r) for r in interior], True)
    convolve([(1, r) for r in interior], True, (1, 2), sums=False)
    convolve([(0, r) for r in interior], True, (2,), sums=False)

    @pl.when(has_last)
    def _():
        top.wait_recv()
        corner_up.start()
        bottom.wait_recv()
        corner_down.start()

    to_up.wait_recv()
    to_down.wait_recv()
    hear(1)
    tell(2)
    clear_rows(2, frames)
    convolve([(t, r) for t in range(2, frames) for r in edges], False)
    for t in range(frames - 1, 1, -1):
        send_stat(t)

    @pl.when(has_last)
    def _():
        late.wait_recv()

    @pl.when(jnp.logical_not(has_last))
    def _():
        xbuf[0:2] = jnp.zeros((2, rows + 2, cols, chans), BF16)

    convolve([(1, r) for r in interior], True, (0,), more=True)
    convolve([(0, r) for r in interior], True, (1,), more=True, sums=False)

    @pl.when(has_last)
    def _():
        corner_up.wait_recv()
        corner_down.wait_recv()

    clear_rows(0, 2)
    convolve([(1, r) for r in edges], False)
    send_stat(1)
    convolve([(0, r) for r in edges], False, (1, 2), sums=False)
    hear(2)
    tell(3)

    @pl.when(has_last)
    def _():
        early.wait_recv()

    hear(3)
    tell(4)
    convolve([(0, r) for r in range(rows)], True, (0,), more=True)
    send_stat(0)
    finish(range(frames - 1, 0, -1))
    rest = pl.ds(head, taken - head)
    total[...] = dot(routes[:, rest], lat[rest])
    finish([0])
    hear(4)
    batch = owners // planes
    turns = [[k for k in order if k < n] for order, n in zip(TURNS, (rows_x, nh, 2))]
    for plane in range(planes):
        z = at_z ^ plane
        here = pl.ds(pl.multiple_of(z * (batch * CAP), batch * CAP), batch * CAP)
        out = dot(routes[here, pl.ds(0, head)], lat[pl.ds(0, head)]) + total[here]
        sides = [
            out[:, k * LANES : (k + 1) * LANES].reshape(batch, CAP, LANES)
            for k in range(width // LANES)
        ]
        pay[pl.ds(z * batch, batch)] = jnp.concatenate(sides, axis=1).astype(BF16)
        for x, h, core in itertools.product(*turns):
            t = (z * rows_x + x) * 2 + core
            k = t * nh + h

            def send():
                pltpu.make_async_remote_copy(
                    src_ref=pay.at[k], dst_ref=arrived.at[me],
                    send_sem=go_sem, recv_sem=come_sem,
                    device_id={"tm": me_t ^ t, "height": me_h ^ h}, device_id_type=MESH,
                ).start()

            if x or h or core:
                send()
            else:
                pl.when(k > 0)(send)
    mine_copy = pltpu.make_async_copy(pay.at[0], arrived.at[me], out_sem)
    mine_copy.start()

    @pl.when(has_next)
    def _():
        for copy in onward:
            copy.wait_send()

    @pl.when(has_last)
    def _():
        corner_up.wait_send()
        corner_down.wait_send()

    to_up.wait_send()
    to_down.wait_send()
    for t in range(frames):
        for k in range(nh - 1):
            stat_copy(t, k).wait_send()
    mine_copy.wait()
    others = pl.ds(0, owners - 1)
    pltpu.make_async_copy(pay.at[others], arrived.at[others], come_sem).wait()
    pltpu.make_async_copy(pay.at[others], arrived.at[others], go_sem).wait()


def compact_kernel(owners, width, arrived, latent_in, routed, latent_out, rows, out, sem):
    latent_copy = pltpu.make_async_copy(latent_in, latent_out, sem.at[0])
    latent_copy.start()
    slots = owners * CAP
    block, chunk = min(LANES, slots), min(2 * LANES, slots)
    tall = arrived[...].astype(F32)
    sides = [
        tall[:, k * CAP : (k + 1) * CAP].reshape(slots, LANES) for k in range(width // LANES)
    ]
    rows[...] = jnp.concatenate(sides, axis=1).astype(BF16)
    pick = onehot(iota((8, LANES), 1) == 0)
    lead = dot_t(pick, rows[:, 0:LANES])
    ahead_of = onehot(iota((block, block), 0) < iota((block, block), 1))
    carry = jnp.zeros((8, 1), F32)
    places = []
    for k in range(slots // block):
        valid = jnp.where(lead[:, k * block : (k + 1) * block] < LIMIT, 1.0, 0.0)
        place = dot(valid.astype(BF16), ahead_of) + carry
        carry = carry + jnp.sum(valid, axis=1, keepdims=True)
        places.append(jnp.where(valid > 0.5, place, -1.0)[0:1].astype(jnp.int32))
    copies = []
    for k in range(slots // chunk):
        at = k * chunk
        line = iota((chunk, block), 0) + at
        chosen = jnp.concatenate(
            [onehot(line == place) for place in places[at // block :]], axis=1
        )
        out[pl.ds(at, chunk)] = dot(chosen, rows[pl.ds(at, slots - at)]).astype(BF16)
        here = pl.ds(at, chunk)
        copies.append(pltpu.make_async_copy(out.at[here], routed.at[here], sem.at[k + 1]))
        copies[-1].start()
    for copy in copies:
        copy.wait()
    latent_copy.wait()


def on_device(
    ntm, nh, video, conv_weight, norm_gain, norm_bias, down_weight, length_table, keep, run_length, owner
):
    frames, rows, cols, chans = video.shape
    width = down_weight.shape[1]
    half_rows, half_cols = rows // 2, cols // 2
    toks = frames * half_rows * half_cols
    owners = ntm * nh
    slots = owners * CAP
    _, taken = heights(half_rows * half_cols, frames)
    ways = (4, 4) if ntm == 32 else (ntm // 2, 1)
    hbm = pl.BlockSpec(memory_space=pltpu.HBM)
    vmem = pl.BlockSpec(memory_space=pltpu.VMEM)
    tiles = CAP * width // LANES
    latent_shape = jax.ShapeDtypeStruct((frames, half_rows * half_cols, width), BF16)
    dma = pltpu.SemaphoreType.DMA
    operands = (
        video,
        conv_weight,
        norm_gain.reshape(1, chans),
        norm_bias.reshape(1, chans),
        down_weight,
        length_table,
        keep,
        run_length,
        owner,
    )
    latent, arrived = pl.pallas_call(
        functools.partial(
            encode_kernel, ntm, nh, (frames, rows, cols, chans, width), ways
        ),
        out_shape=(latent_shape, jax.ShapeDtypeStruct((owners, tiles, LANES), BF16)),
        in_specs=[hbm] * 9,
        out_specs=(vmem, vmem),
        scratch_shapes=[
            pltpu.VMEM((frames + 2, rows + 2, cols, chans), BF16),
            pltpu.VMEM((3, 3, chans, 2 * chans), BF16),
            pltpu.VMEM((3, 4, chans, 2 * chans), BF16),
            pltpu.VMEM((1, chans), F32),
            pltpu.VMEM((1, chans), F32),
            pltpu.VMEM(down_weight.shape, BF16),
            pltpu.VMEM(length_table.shape, F32),
            pltpu.VMEM(keep.shape, jnp.int32),
            pltpu.VMEM(keep.shape, jnp.int32),
            pltpu.VMEM(keep.shape, jnp.int32),
            pltpu.VMEM((frames, rows, cols, chans), F32),
            pltpu.VMEM((nh, frames, 16, chans), F32),
            pltpu.VMEM((slots, taken), BF16),
            pltpu.VMEM((taken, width), F32),
            pltpu.VMEM((taken, width), BF16),
            pltpu.VMEM((slots, width), F32),
            pltpu.VMEM((owners, tiles, LANES), BF16),
            dma((12,)),
            dma((8,)),
            dma((8,)),
            dma((frames, nh - 1)),
            dma((frames, nh)),
            pltpu.SemaphoreType.REGULAR((5,)),
            dma,
            dma,
            dma,
        ],
        compiler_params=pltpu.CompilerParams(
            collective_id=0, has_side_effects=True, vmem_limit_bytes=48 * 1024 * 1024
        ),
        name="encode",
    )(*(pltpu.with_memory_space_constraint(array, pltpu.HBM) for array in operands))
    routed, latent = pl.pallas_call(
        functools.partial(compact_kernel, owners, width),
        out_shape=(jax.ShapeDtypeStruct((slots, width), BF16), latent_shape),
        in_specs=[vmem, hbm],
        out_specs=(hbm, hbm),
        scratch_shapes=[
            pltpu.VMEM((slots, width), BF16),
            pltpu.VMEM((slots, width), BF16),
            dma((5,)),
        ],
        compiler_params=pltpu.CompilerParams(vmem_limit_bytes=48 * 1024 * 1024),
        name="compact",
    )(arrived, latent)
    return latent.reshape(frames, half_rows, half_cols, width), routed


def solution(mesh):
    return jax.shard_map(
        functools.partial(on_device, mesh.shape["tm"], mesh.shape["height"]),
        mesh=mesh,
        in_specs=(
            P("tm", "height", None, None),
            P(),
            P(),
            P(),
            P(),
            P(),
            P("tm", "height", None),
            P("tm", "height", None),
            P("tm", "height", None),
        ),
        out_specs=(P("tm", "height", None, None), P(("tm", "height"), None)),
        check_vma=False,
    )
```

```python
import functools
import itertools

import jax
import jax.numpy as jnp
from jax import lax
from jax.experimental import pallas as pl
from jax.experimental.pallas import tpu as pltpu
from jax.sharding import PartitionSpec as P

GROUPS = 32
LMAX = 8
CAP = 8
EPSILON = 1e-06
LANES = 128
TURNS = ((2, 3, 1, 0), (2, 3, 1, 0), (1, 0))
EMPTY = 2.0**127
LIMIT = 2.0**126
MESH = pl.DeviceIdType.MESH
F32 = jnp.float32
BF16 = jnp.bfloat16


def dot(a, b):
    return jnp.dot(a, b, preferred_element_type=F32)


def dot_t(a, b, precision=None):
    return lax.dot_general(
        a, b, (((1,), (1,)), ((), ())), preferred_element_type=F32, precision=precision
    )


def iota(shape, dim):
    return lax.broadcasted_iota(jnp.int32, shape, dim)


def onehot(mask):
    return jnp.where(mask, 1.0, 0.0).astype(BF16)


def heights(patches, frames):
    head = (patches // LANES + 1) * LANES
    return head, head + -(-(frames - 1) * patches // LANES) * LANES


def encode_kernel(
    ntm, nh, shapes, ways,
    video_in, weight_in, gain_in, bias_in, down_in, table_in, keep_in, run_in, owner_in,
    latent_out, arrived,
    xbuf, wpair, wlast, gain, bias, down, table, keep, run, owner,
    hidden, stat, routes, extra, lat, total, pay,
    in_sem, halo_send, halo_recv, stat_send, stat_recv, ready, out_sem, go_sem, come_sem,
):
    frames, rows, cols, chans, width = shapes
    half_rows, half_cols = rows // 2, cols // 2
    patches = half_rows * half_cols
    toks = frames * patches
    owners = ntm * nh
    slots = owners * CAP
    head, taken = heights(patches, frames)
    me_t, me_h = lax.axis_index("tm"), lax.axis_index("height")
    me = me_t * nh + me_h
    next_t, last_t = lax.rem(me_t + 1, ntm), lax.rem(me_t + ntm - 1, ntm)
    up, down_h = lax.rem(me_h + nh - 1, nh), lax.rem(me_h + 1, nh)
    peers = [lax.rem(me_h + k, nh) for k in range(1, nh)]

    rows_x, planes = ways
    assert owners == 2 * nh * rows_x * planes and all(n & (n - 1) == 0 for n in (nh, *ways))

    even = lax.rem(me_t, 2) == 0
    has_next, has_last = me_t < ntm - 1, me_t > 0

    def signal(semaphore, t, h):
        pl.semaphore_signal(
            semaphore, inc=1, device_id={"tm": t, "height": h}, device_id_type=MESH
        )

    at_x, at_z = lax.rem(me_t // 2, rows_x), me_t // (2 * rows_x)
    first_x = even & (at_x == 0)
    first_z = first_x & (at_z == 0)
    later_x, later_z = even & (at_x > 0), first_x & (at_z > 0)
    to_first_x, to_first_z = me_t - 2 * at_x, 0
    all_x = [me_t + 2 * k for k in range(1, rows_x)]
    all_z = [2 * rows_x * k for k in range(1, planes)]
    relay = [
        (even, [(me_t, h) for h in peers], even, nh - 1),
        (later_x, [(to_first_x, me_h)], first_x, rows_x - 1),
        (later_z, [(to_first_z, me_h)], first_z, planes - 1),
        (first_z, [(t, me_h) for t in all_z], later_z, 1),
        (first_x, [(me_t + k, me_h) for k in range(1, 2 * rows_x)], jnp.logical_not(first_x), 1),
    ]
    barrier = pltpu.get_barrier_semaphore()

    @pl.when(has_last)
    def _():
        signal(barrier, last_t, me_h)

    for h in peers:
        signal(barrier, me_t, h)

    @pl.when(first_x)
    def _():
        for t in all_x:
            signal(barrier, t, me_h)

    @pl.when(first_z)
    def _():
        for t in all_z:
            signal(barrier, t, me_h)

    loads = [
        (keep_in, keep), (run_in, run), (owner_in, owner), (table_in, table),
        (video_in, xbuf.at[pl.ds(2, frames), pl.ds(1, rows)]),
        (weight_in.at[:, :, 0], wpair.at[:, :, :, pl.ds(0, chans)]),
        (weight_in.at[:, :, 1], wpair.at[:, :, :, pl.ds(chans, chans)]),
        (weight_in.at[:, :, 2], wlast.at[:, pl.ds(0, 3), :, pl.ds(0, chans)]),
        (weight_in.at[:, :, 2], wlast.at[:, pl.ds(1, 3), :, pl.ds(chans, chans)]),
        (down_in, down), (gain_in, gain), (bias_in, bias),
    ]
    loads = [
        pltpu.make_async_copy(src, dst, in_sem.at[k]) for k, (src, dst) in enumerate(loads)
    ]
    for copy in loads:
        copy.start()
    wlast[:, 3, :, pl.ds(0, chans)] = jnp.zeros((3, chans, chans), BF16)
    wlast[:, 0, :, pl.ds(chans, chans)] = jnp.zeros((3, chans, chans), BF16)
    awaited = nh - 1 + jnp.where(has_next, 1, 0)
    pl.semaphore_wait(barrier, awaited + jnp.where(later_x | later_z, 1, 0))

    def halo(k, src, dst, t, h):
        return pltpu.make_async_remote_copy(
            src_ref=src, dst_ref=dst, send_sem=halo_send.at[k], recv_sem=halo_recv.at[k],
            device_id={"tm": t, "height": h}, device_id_type=MESH,
        )

    pair = pl.ds(frames - 2, 2)
    inner = pl.ds(1, rows - 2)
    to_up = halo(0, video_in.at[:, 0], xbuf.at[pl.ds(2, frames), rows + 1], me_t, up)
    to_down = halo(1, video_in.at[:, rows - 1], xbuf.at[pl.ds(2, frames), 0], me_t, down_h)
    top = halo(2, video_in.at[pair, 0], xbuf.at[pl.ds(0, 2), 1], next_t, me_h)
    bottom = halo(3, video_in.at[pair, rows - 1], xbuf.at[pl.ds(0, 2), rows], next_t, me_h)
    late = halo(4, video_in.at[frames - 1, inner], xbuf.at[1, pl.ds(2, rows - 2)], next_t, me_h)
    early = halo(5, video_in.at[frames - 2, inner], xbuf.at[0, pl.ds(2, rows - 2)], next_t, me_h)
    corner_up = halo(6, xbuf.at[pl.ds(0, 2), 1], xbuf.at[pl.ds(0, 2), rows + 1], me_t, up)
    corner_down = halo(7, xbuf.at[pl.ds(0, 2), rows], xbuf.at[pl.ds(0, 2), 0], me_t, down_h)
    onward = (top, bottom, late, early)

    @pl.when(has_next)
    def _():
        for copy in onward[:2]:
            copy.start()

    to_up.start()
    to_down.start()

    @pl.when(has_next)
    def _():
        for copy in onward[2:]:
            copy.start()

    def tell(k):
        if k in (0, 4) or (rows_x, planes)[k in (2, 3)] > 1:

            @pl.when(relay[k][0])
            def _():
                for t, h in relay[k][1]:
                    signal(ready.at[k], t, h)

    def hear(k):
        if k in (0, 4) or (rows_x, planes)[k in (2, 3)] > 1:

            @pl.when(relay[k][2])
            def _():
                pl.semaphore_wait(ready.at[k], relay[k][3])

    tell(0)
    for copy in loads[:4]:
        copy.wait()
    def along(pieces, filler):
        row = [pieces[r] for r in range(half_rows)]
        row += [jnp.full((1, head - patches), filler, jnp.int32)]
        row += [pieces[r] for r in range(half_rows, frames * half_rows)]
        row += [jnp.full((1, taken - head - (toks - patches)), filler, jnp.int32)]
        return jnp.concatenate([piece for piece in row if piece.shape[1]], axis=1)

    lines = [(t, slice(r, r + 1)) for t in range(frames) for r in range(half_rows)]
    place = []
    for t, r in lines:
        place.append(jnp.where(keep[t, r] == 1, owner[t, r] ^ me, -1))
    place = along(place, -1)
    length = along([run[t, r] - 1 for t, r in lines], -1)
    member = iota((owners, taken), 0) == place
    before_lane = onehot(iota((LANES, LANES), 0) < iota((LANES, LANES), 1))
    kept = jnp.zeros((owners, 1), F32)
    for k in range(taken // LANES):
        at = slice(k * LANES, (k + 1) * LANES)
        block = jnp.where(member[:, at], 1.0, 0.0)
        ahead = dot(block.astype(BF16), before_lane) + kept
        kept = kept + jnp.sum(block, axis=1, keepdims=True)
        rank = jnp.sum(ahead * block, axis=0, keepdims=True).astype(jnp.int32)
        slot = jnp.where(place[:, at] < 0, -1, place[:, at] * CAP + rank)
        chosen = iota((slots, LANES), 0) == slot
        if k == patches // LANES:
            partly = chosen
        else:
            routes[:, at] = onehot(chosen)
    at = slice(patches // LANES * LANES, (patches // LANES + 1) * LANES)
    unused = iota((owners, CAP, LANES), 1).astype(F32) >= kept.reshape(owners, 1, 1)
    mark = unused & (iota((owners, CAP, LANES), 2) == patches % LANES)
    routes[:, at] = jnp.maximum(
        onehot(partly).astype(F32), jnp.where(mark, 1.0, 0.0).reshape(slots, LANES)
    ).astype(BF16)
    lat[pl.ds(patches, head - patches)] = jnp.where(
        iota((head - patches, width), 0) == 0, EMPTY, 0.0
    ).astype(BF16)
    if taken > head + toks - patches:
        tail = taken - head - (toks - patches)
        lat[pl.ds(taken - tail, tail)] = jnp.zeros((tail, width), BF16)
    row_of = iota((4 * LMAX, taken), 0)
    which = (lax.rem(row_of, LMAX) == length) & (row_of < 3 * LMAX)
    which = jnp.where(which, 1.0, 0.0).T.astype(BF16)
    part0 = table[...].astype(BF16)
    rest = table[...] - part0.astype(F32)
    part1 = rest.astype(BF16)
    part2 = (rest - part1.astype(F32)).astype(BF16)
    parts = jnp.concatenate(
        [part0.astype(F32), part1.astype(F32), part2.astype(F32), jnp.zeros((LMAX, width), F32)],
        axis=0,
    ).astype(BF16)
    extra[...] = dot(which, parts)

    for copy in loads[4:]:
        copy.wait()
    hear(0)
    tell(1)

    first = iota((1, 8, chans), 1) == 0
    final = iota((1, 8, chans), 1) == 7

    def gather(lines, a, b):
        return jnp.concatenate([xbuf[t + a, r + b] for t, r in lines], axis=0)

    def convolve(lines, paired, afters=(0, 1, 2), more=False, sums=True):
        count = len(lines)
        window = jnp.concatenate(
            [gather(lines, a, b) for a in afters for b in range(3)], axis=1
        )
        used = slice(afters[0], afters[-1] + 1)
        taps = dot(window, wpair[used].reshape(-1, 2 * chans))
        left = pltpu.roll(taps[:, :chans], 1, 0).reshape(count, cols, chans)
        left = jnp.concatenate([jnp.where(first, 0.0, left[:, :8]), left[:, 8:]], axis=1)
        out = taps[:, chans:].reshape(count, cols, chans) + left
        if paired:
            half = count // 2
            window = jnp.concatenate(
                [gather(lines[::2], a, b) for a in afters for b in range(4)], axis=1
            )
            taps = dot(window, wlast[used].reshape(-1, 2 * chans))
            right = jnp.concatenate(
                [
                    pltpu.roll(
                        taps[:, k * chans : (k + 1) * chans], half * cols - 1, 0
                    ).reshape(half, 1, cols, chans)
                    for k in range(2)
                ],
                axis=1,
            )
        else:
            taps = dot(window, wlast[used, 0:3, :, 0:chans].reshape(-1, chans))
            right = pltpu.roll(taps, count * cols - 1, 0)
        right = right.reshape(count, cols, chans)
        out = out + jnp.concatenate(
            [right[:, :-8], jnp.where(final, 0.0, right[:, -8:])], axis=1
        )
        for t in sorted({t for t, _ in lines}):
            mine = [k for k, line in enumerate(lines) if line[0] == t]
            part = out[mine[0] : mine[-1] + 1]
            if more:
                part = part + hidden[t, pl.ds(lines[mine[0]][1], len(mine))]
            for k in mine:
                hidden[t, lines[k][1]] = part[k - mine[0]]
            if not sums:
                continue
            tiles = part.reshape(len(mine) * cols // 8, 8, chans)
            total, square = jnp.sum(tiles, axis=0), jnp.sum(tiles * tiles, axis=0)
            if not paired:
                total = total + stat[me_h, t, pl.ds(0, 8)]
                square = square + stat[me_h, t, pl.ds(8, 8)]
            stat[me_h, t, pl.ds(0, 8)] = total
            stat[me_h, t, pl.ds(8, 8)] = square

    def clear_rows(at, count):
        @pl.when(me_h == 0)
        def _():
            xbuf[pl.ds(at, count), 0] = jnp.zeros((count, cols, chans), BF16)

        @pl.when(me_h == nh - 1)
        def _():
            xbuf[pl.ds(at, count), rows + 1] = jnp.zeros((count, cols, chans), BF16)

    def stat_copy(t, k):
        return pltpu.make_async_remote_copy(
            src_ref=stat.at[me_h, t], dst_ref=stat.at[me_h, t],
            send_sem=stat_send.at[t, k], recv_sem=stat_recv.at[t, me_h],
            device_id={"tm": me_t, "height": peers[k]}, device_id_type=MESH,
        )

    def stat_arrival(t, k):
        return pltpu.make_async_remote_copy(
            src_ref=stat.at[peers[k], t], dst_ref=stat.at[peers[k], t],
            send_sem=stat_send.at[t, k], recv_sem=stat_recv.at[t, peers[k]],
            device_id={"tm": me_t, "height": peers[k]}, device_id_type=MESH,
        )

    def send_stat(t):
        for k in sorted(range(nh - 1), key=lambda k: -min(k + 1, nh - k - 1)):
            stat_copy(t, k).start()

    group_of = chans // GROUPS
    same = onehot(iota((chans, chans), 0) // group_of == iota((chans, chans), 1) // group_of)
    count = rows * nh * cols * group_of

    def finish(times):
        for t in times:
            for k in range(nh - 1):
                stat_arrival(t, k).wait_recv()
        sums = [
            jnp.sum(jnp.sum(stat[:, t], axis=0).reshape(2, 8, chans), axis=1) for t in times
        ]
        sums = jnp.concatenate(sums + [jnp.zeros((8 - 2 * len(times), chans), F32)], axis=0)
        part0 = sums.astype(BF16).astype(F32)
        part1 = (sums - part0).astype(BF16).astype(F32)
        parts = jnp.concatenate([part0, part1, sums - part0 - part1], axis=0).astype(BF16)
        grouped = dot(parts, same)
        grouped = (grouped[0:8] + grouped[8:16] + grouped[16:24]) / count
        for k, t in enumerate(times):
            average, squares = grouped[2 * k : 2 * k + 1], grouped[2 * k + 1 : 2 * k + 2]
            spread = squares - average * average
            finish_frame(t, average, 0.5 * (lax.rsqrt(spread + EPSILON) * gain[...]))

    def finish_frame(t, average, scale):
        shift = 0.5 * bias[...]

        def act(r, b):
            h = hidden[t, r, pl.ds(b, half_cols, stride=2), :]
            v = (h - average) * scale + shift
            return (v + v * jnp.tanh(v)).astype(BF16)

        merged = jnp.concatenate(
            [
                jnp.concatenate(
                    [act(2 * i + a, b) for a in range(2) for b in range(2)], axis=1
                )
                for i in range(half_rows)
            ],
            axis=0,
        )
        latent = dot(merged, down[...]).astype(BF16)
        latent_out[t] = latent
        at = pl.ds(0 if t == 0 else head + (t - 1) * patches, patches)
        lat[at] = (latent.astype(F32) + extra[at]).astype(BF16)

    interior, edges = range(1, rows - 1), (0, rows - 1)
    for t in range(frames - 1, 1, -1):
        convolve([(t, r) for r in interior], True)
    convolve([(1, r) for r in interior], True, (1, 2), sums=False)
    convolve([(0, r) for r in interior], True, (2,), sums=False)

    @pl.when(has_last)
    def _():
        top.wait_recv()
        corner_up.start()
        bottom.wait_recv()
        corner_down.start()

    to_up.wait_recv()
    to_down.wait_recv()
    hear(1)
    tell(2)
    clear_rows(2, frames)
    convolve([(t, r) for t in range(2, frames) for r in edges], False)
    for t in range(frames - 1, 1, -1):
        send_stat(t)

    @pl.when(has_last)
    def _():
        late.wait_recv()

    @pl.when(jnp.logical_not(has_last))
    def _():
        xbuf[0:2] = jnp.zeros((2, rows + 2, cols, chans), BF16)

    convolve([(1, r) for r in interior], True, (0,), more=True)
    convolve([(0, r) for r in interior], True, (1,), more=True, sums=False)

    @pl.when(has_last)
    def _():
        corner_up.wait_recv()
        corner_down.wait_recv()

    clear_rows(0, 2)
    convolve([(1, r) for r in edges], False)
    send_stat(1)
    convolve([(0, r) for r in edges], False, (1, 2), sums=False)
    hear(2)
    tell(3)

    @pl.when(has_last)
    def _():
        early.wait_recv()

    convolve([(0, r) for r in range(rows)], True, (0,), more=True)
    send_stat(0)
    hear(3)
    tell(4)
    finish(range(frames - 1, 1, -1))
    finish([1])
    rest = pl.ds(head, taken - head)
    total[...] = dot(routes[:, rest], lat[rest])
    finish([0])
    hear(4)
    batch = owners // planes
    turns = [[k for k in order if k < n] for order, n in zip(TURNS, (rows_x, nh, 2))]
    for plane in range(planes):
        z = at_z ^ plane
        here = pl.ds(pl.multiple_of(z * (batch * CAP), batch * CAP), batch * CAP)
        out = dot(routes[here, pl.ds(0, head)], lat[pl.ds(0, head)]) + total[here]
        sides = [
            out[:, k * LANES : (k + 1) * LANES].reshape(batch, CAP, LANES)
            for k in range(width // LANES)
        ]
        pay[pl.ds(z * batch, batch)] = jnp.concatenate(sides, axis=1).astype(BF16)
        for x, h, core in itertools.product(*turns):
            t = (z * rows_x + x) * 2 + core
            k = t * nh + h

            def send():
                pltpu.make_async_remote_copy(
                    src_ref=pay.at[k], dst_ref=arrived.at[me],
                    send_sem=go_sem, recv_sem=come_sem,
                    device_id={"tm": me_t ^ t, "height": me_h ^ h}, device_id_type=MESH,
                ).start()

            if x or h or core:
                send()
            else:
                pl.when(k > 0)(send)
    mine_copy = pltpu.make_async_copy(pay.at[0], arrived.at[me], out_sem)
    mine_copy.start()

    @pl.when(has_next)
    def _():
        for copy in onward:
            copy.wait_send()

    @pl.when(has_last)
    def _():
        corner_up.wait_send()
        corner_down.wait_send()

    to_up.wait_send()
    to_down.wait_send()
    for t in range(frames):
        for k in range(nh - 1):
            stat_copy(t, k).wait_send()
    mine_copy.wait()
    others = pl.ds(0, owners - 1)
    pltpu.make_async_copy(pay.at[others], arrived.at[others], come_sem).wait()
    pltpu.make_async_copy(pay.at[others], arrived.at[others], go_sem).wait()


def compact_kernel(owners, width, arrived, latent_in, routed, latent_out, rows, out, sem):
    latent_copy = pltpu.make_async_copy(latent_in, latent_out, sem.at[0])
    latent_copy.start()
    slots = owners * CAP
    block, chunk = min(LANES, slots), min(2 * LANES, slots)
    tall = arrived[...].astype(F32)
    sides = [
        tall[:, k * CAP : (k + 1) * CAP].reshape(slots, LANES) for k in range(width // LANES)
    ]
    rows[...] = jnp.concatenate(sides, axis=1).astype(BF16)
    pick = onehot(iota((8, LANES), 1) == 0)
    lead = dot_t(pick, rows[:, 0:LANES])
    ahead_of = onehot(iota((block, block), 0) < iota((block, block), 1))
    carry = jnp.zeros((8, 1), F32)
    places = []
    for k in range(slots // block):
        valid = jnp.where(lead[:, k * block : (k + 1) * block] < LIMIT, 1.0, 0.0)
        place = dot(valid.astype(BF16), ahead_of) + carry
        carry = carry + jnp.sum(valid, axis=1, keepdims=True)
        places.append(jnp.where(valid > 0.5, place, -1.0)[0:1].astype(jnp.int32))
    copies = []
    for k in range(slots // chunk):
        at = k * chunk
        line = iota((chunk, block), 0) + at
        chosen = jnp.concatenate(
            [onehot(line == place) for place in places[at // block :]], axis=1
        )
        out[pl.ds(at, chunk)] = dot(chosen, rows[pl.ds(at, slots - at)]).astype(BF16)
        here = pl.ds(at, chunk)
        copies.append(pltpu.make_async_copy(out.at[here], routed.at[here], sem.at[k + 1]))
        copies[-1].start()
    for copy in copies:
        copy.wait()
    latent_copy.wait()


def on_device(
    ntm, nh, video, conv_weight, norm_gain, norm_bias, down_weight, length_table, keep, run_length, owner
):
    frames, rows, cols, chans = video.shape
    width = down_weight.shape[1]
    half_rows, half_cols = rows // 2, cols // 2
    toks = frames * half_rows * half_cols
    owners = ntm * nh
    slots = owners * CAP
    _, taken = heights(half_rows * half_cols, frames)
    ways = (4, 4) if ntm == 32 else (ntm // 2, 1)
    hbm = pl.BlockSpec(memory_space=pltpu.HBM)
    vmem = pl.BlockSpec(memory_space=pltpu.VMEM)
    tiles = CAP * width // LANES
    latent_shape = jax.ShapeDtypeStruct((frames, half_rows * half_cols, width), BF16)
    dma = pltpu.SemaphoreType.DMA
    operands = (
        video,
        conv_weight,
        norm_gain.reshape(1, chans),
        norm_bias.reshape(1, chans),
        down_weight,
        length_table,
        keep,
        run_length,
        owner,
    )
    latent, arrived = pl.pallas_call(
        functools.partial(
            encode_kernel, ntm, nh, (frames, rows, cols, chans, width), ways
        ),
        out_shape=(latent_shape, jax.ShapeDtypeStruct((owners, tiles, LANES), BF16)),
        in_specs=[hbm] * 9,
        out_specs=(vmem, vmem),
        scratch_shapes=[
            pltpu.VMEM((frames + 2, rows + 2, cols, chans), BF16),
            pltpu.VMEM((3, 3, chans, 2 * chans), BF16),
            pltpu.VMEM((3, 4, chans, 2 * chans), BF16),
            pltpu.VMEM((1, chans), F32),
            pltpu.VMEM((1, chans), F32),
            pltpu.VMEM(down_weight.shape, BF16),
            pltpu.VMEM(length_table.shape, F32),
            pltpu.VMEM(keep.shape, jnp.int32),
            pltpu.VMEM(keep.shape, jnp.int32),
            pltpu.VMEM(keep.shape, jnp.int32),
            pltpu.VMEM((frames, rows, cols, chans), F32),
            pltpu.VMEM((nh, frames, 16, chans), F32),
            pltpu.VMEM((slots, taken), BF16),
            pltpu.VMEM((taken, width), F32),
            pltpu.VMEM((taken, width), BF16),
            pltpu.VMEM((slots, width), F32),
            pltpu.VMEM((owners, tiles, LANES), BF16),
            dma((12,)),
            dma((8,)),
            dma((8,)),
            dma((frames, nh - 1)),
            dma((frames, nh)),
            pltpu.SemaphoreType.REGULAR((5,)),
            dma,
            dma,
            dma,
        ],
        compiler_params=pltpu.CompilerParams(
            collective_id=0, has_side_effects=True, vmem_limit_bytes=48 * 1024 * 1024
        ),
        name="encode",
    )(*(pltpu.with_memory_space_constraint(array, pltpu.HBM) for array in operands))
    routed, latent = pl.pallas_call(
        functools.partial(compact_kernel, owners, width),
        out_shape=(jax.ShapeDtypeStruct((slots, width), BF16), latent_shape),
        in_specs=[vmem, hbm],
        out_specs=(hbm, hbm),
        scratch_shapes=[
            pltpu.VMEM((slots, width), BF16),
            pltpu.VMEM((slots, width), BF16),
            dma((5,)),
        ],
        compiler_params=pltpu.CompilerParams(vmem_limit_bytes=48 * 1024 * 1024),
        name="compact",
    )(arrived, latent)
    return latent.reshape(frames, half_rows, half_cols, width), routed


def solution(mesh):
    return jax.shard_map(
        functools.partial(on_device, mesh.shape["tm"], mesh.shape["height"]),
        mesh=mesh,
        in_specs=(
            P("tm", "height", None, None),
            P(),
            P(),
            P(),
            P(),
            P(),
            P("tm", "height", None),
            P("tm", "height", None),
            P("tm", "height", None),
        ),
        out_specs=(P("tm", "height", None, None), P(("tm", "height"), None)),
        check_vma=False,
    )
```

```python
import functools
import itertools

import jax
import jax.numpy as jnp
from jax import lax
from jax.experimental import pallas as pl
from jax.experimental.pallas import tpu as pltpu
from jax.sharding import PartitionSpec as P

GROUPS = 32
LMAX = 8
CAP = 8
EPSILON = 1e-06
LANES = 128
TURNS = ((2, 3, 1, 0), (2, 3, 1, 0), (1, 0))
EMPTY = 2.0**127
LIMIT = 2.0**126
MESH = pl.DeviceIdType.MESH
F32 = jnp.float32
BF16 = jnp.bfloat16


def dot(a, b):
    return jnp.dot(a, b, preferred_element_type=F32)


def dot_t(a, b, precision=None):
    return lax.dot_general(
        a, b, (((1,), (1,)), ((), ())), preferred_element_type=F32, precision=precision
    )


def iota(shape, dim):
    return lax.broadcasted_iota(jnp.int32, shape, dim)


def onehot(mask):
    return jnp.where(mask, 1.0, 0.0).astype(BF16)


def heights(patches, frames):
    head = (patches // LANES + 1) * LANES
    return head, head + -(-(frames - 1) * patches // LANES) * LANES


def encode_kernel(
    ntm, nh, shapes, ways,
    video_in, weight_in, gain_in, bias_in, down_in, table_in, keep_in, run_in, owner_in,
    latent_out, arrived,
    xbuf, wpair, wlast, gain, bias, down, table, keep, run, owner,
    hidden, stat, routes, extra, lat, total, pay,
    in_sem, halo_send, halo_recv, stat_send, stat_recv, ready, out_sem, go_sem, come_sem,
):
    frames, rows, cols, chans, width = shapes
    half_rows, half_cols = rows // 2, cols // 2
    patches = half_rows * half_cols
    toks = frames * patches
    owners = ntm * nh
    slots = owners * CAP
    head, taken = heights(patches, frames)
    me_t, me_h = lax.axis_index("tm"), lax.axis_index("height")
    me = me_t * nh + me_h
    next_t, last_t = lax.rem(me_t + 1, ntm), lax.rem(me_t + ntm - 1, ntm)
    up, down_h = lax.rem(me_h + nh - 1, nh), lax.rem(me_h + 1, nh)
    peers = [lax.rem(me_h + k, nh) for k in range(1, nh)]

    rows_x, planes = ways
    assert owners == 2 * nh * rows_x * planes and all(n & (n - 1) == 0 for n in (nh, *ways))

    even = lax.rem(me_t, 2) == 0
    has_next, has_last = me_t < ntm - 1, me_t > 0

    def signal(semaphore, t, h):
        pl.semaphore_signal(
            semaphore, inc=1, device_id={"tm": t, "height": h}, device_id_type=MESH
        )

    at_x, at_z = lax.rem(me_t // 2, rows_x), me_t // (2 * rows_x)
    first_x = even & (at_x == 0)
    first_z = first_x & (at_z == 0)
    later_x, later_z = even & (at_x > 0), first_x & (at_z > 0)
    to_first_x, to_first_z = me_t - 2 * at_x, 0
    all_x = [me_t + 2 * k for k in range(1, rows_x)]
    all_z = [2 * rows_x * k for k in range(1, planes)]
    relay = [
        (even, [(me_t, h) for h in peers], even, nh - 1),
        (later_x, [(to_first_x, me_h)], first_x, rows_x - 1),
        (later_z, [(to_first_z, me_h)], first_z, planes - 1),
        (first_z, [(t, me_h) for t in all_z], later_z, 1),
        (first_x, [(me_t + k, me_h) for k in range(1, 2 * rows_x)], jnp.logical_not(first_x), 1),
    ]
    barrier = pltpu.get_barrier_semaphore()

    @pl.when(has_last)
    def _():
        signal(barrier, last_t, me_h)

    for h in peers:
        signal(barrier, me_t, h)

    @pl.when(first_x)
    def _():
        for t in all_x:
            signal(barrier, t, me_h)

    @pl.when(first_z)
    def _():
        for t in all_z:
            signal(barrier, t, me_h)

    loads = [
        (keep_in, keep), (run_in, run), (owner_in, owner), (table_in, table),
        (video_in, xbuf.at[pl.ds(2, frames), pl.ds(1, rows)]),
        (weight_in.at[:, :, 0], wpair.at[:, :, :, pl.ds(0, chans)]),
        (weight_in.at[:, :, 1], wpair.at[:, :, :, pl.ds(chans, chans)]),
        (weight_in.at[:, :, 2], wlast.at[:, pl.ds(0, 3), :, pl.ds(0, chans)]),
        (weight_in.at[:, :, 2], wlast.at[:, pl.ds(1, 3), :, pl.ds(chans, chans)]),
        (down_in, down), (gain_in, gain), (bias_in, bias),
    ]
    loads = [
        pltpu.make_async_copy(src, dst, in_sem.at[k]) for k, (src, dst) in enumerate(loads)
    ]
    for copy in loads:
        copy.start()
    wlast[:, 3, :, pl.ds(0, chans)] = jnp.zeros((3, chans, chans), BF16)
    wlast[:, 0, :, pl.ds(chans, chans)] = jnp.zeros((3, chans, chans), BF16)
    awaited = nh - 1 + jnp.where(has_next, 1, 0)
    pl.semaphore_wait(barrier, awaited + jnp.where(later_x | later_z, 1, 0))

    def halo(k, src, dst, t, h):
        return pltpu.make_async_remote_copy(
            src_ref=src, dst_ref=dst, send_sem=halo_send.at[k], recv_sem=halo_recv.at[k],
            device_id={"tm": t, "height": h}, device_id_type=MESH,
        )

    pair = pl.ds(frames - 2, 2)
    inner = pl.ds(1, rows - 2)
    to_up = halo(0, video_in.at[:, 0], xbuf.at[pl.ds(2, frames), rows + 1], me_t, up)
    to_down = halo(1, video_in.at[:, rows - 1], xbuf.at[pl.ds(2, frames), 0], me_t, down_h)
    top = halo(2, video_in.at[pair, 0], xbuf.at[pl.ds(0, 2), 1], next_t, me_h)
    bottom = halo(3, video_in.at[pair, rows - 1], xbuf.at[pl.ds(0, 2), rows], next_t, me_h)
    late = halo(4, video_in.at[frames - 1, inner], xbuf.at[1, pl.ds(2, rows - 2)], next_t, me_h)
    early = halo(5, video_in.at[frames - 2, inner], xbuf.at[0, pl.ds(2, rows - 2)], next_t, me_h)
    corner_up = halo(6, xbuf.at[pl.ds(0, 2), 1], xbuf.at[pl.ds(0, 2), rows + 1], me_t, up)
    corner_down = halo(7, xbuf.at[pl.ds(0, 2), rows], xbuf.at[pl.ds(0, 2), 0], me_t, down_h)
    onward = (top, bottom, late, early)

    @pl.when(has_next)
    def _():
        for copy in onward[:2]:
            copy.start()

    to_up.start()
    to_down.start()

    @pl.when(has_next)
    def _():
        for copy in onward[2:]:
            copy.start()

    def tell(k):
        if k in (0, 4) or (rows_x, planes)[k in (2, 3)] > 1:

            @pl.when(relay[k][0])
            def _():
                for t, h in relay[k][1]:
                    signal(ready.at[k], t, h)

    def hear(k):
        if k in (0, 4) or (rows_x, planes)[k in (2, 3)] > 1:

            @pl.when(relay[k][2])
            def _():
                pl.semaphore_wait(ready.at[k], relay[k][3])

    tell(0)
    for copy in loads[:4]:
        copy.wait()
    def along(pieces, filler):
        row = [pieces[r] for r in range(half_rows)]
        row += [jnp.full((1, head - patches), filler, jnp.int32)]
        row += [pieces[r] for r in range(half_rows, frames * half_rows)]
        row += [jnp.full((1, taken - head - (toks - patches)), filler, jnp.int32)]
        return jnp.concatenate([piece for piece in row if piece.shape[1]], axis=1)

    lines = [(t, slice(r, r + 1)) for t in range(frames) for r in range(half_rows)]
    place = []
    for t, r in lines:
        place.append(jnp.where(keep[t, r] == 1, owner[t, r] ^ me, -1))
    place = along(place, -1)
    length = along([run[t, r] - 1 for t, r in lines], -1)
    member = iota((owners, taken), 0) == place
    before_lane = onehot(iota((LANES, LANES), 0) < iota((LANES, LANES), 1))
    kept = jnp.zeros((owners, 1), F32)
    for k in range(taken // LANES):
        at = slice(k * LANES, (k + 1) * LANES)
        block = jnp.where(member[:, at], 1.0, 0.0)
        ahead = dot(block.astype(BF16), before_lane) + kept
        kept = kept + jnp.sum(block, axis=1, keepdims=True)
        rank = jnp.sum(ahead * block, axis=0, keepdims=True).astype(jnp.int32)
        slot = jnp.where(place[:, at] < 0, -1, place[:, at] * CAP + rank)
        chosen = iota((slots, LANES), 0) == slot
        if k == patches // LANES:
            partly = chosen
        else:
            routes[:, at] = onehot(chosen)
    at = slice(patches // LANES * LANES, (patches // LANES + 1) * LANES)
    unused = iota((owners, CAP, LANES), 1).astype(F32) >= kept.reshape(owners, 1, 1)
    mark = unused & (iota((owners, CAP, LANES), 2) == patches % LANES)
    routes[:, at] = jnp.maximum(
        onehot(partly).astype(F32), jnp.where(mark, 1.0, 0.0).reshape(slots, LANES)
    ).astype(BF16)
    lat[pl.ds(patches, head - patches)] = jnp.where(
        iota((head - patches, width), 0) == 0, EMPTY, 0.0
    ).astype(BF16)
    if taken > head + toks - patches:
        tail = taken - head - (toks - patches)
        lat[pl.ds(taken - tail, tail)] = jnp.zeros((tail, width), BF16)
    row_of = iota((4 * LMAX, taken), 0)
    which = (lax.rem(row_of, LMAX) == length) & (row_of < 3 * LMAX)
    which = jnp.where(which, 1.0, 0.0).T.astype(BF16)
    part0 = table[...].astype(BF16)
    rest = table[...] - part0.astype(F32)
    part1 = rest.astype(BF16)
    part2 = (rest - part1.astype(F32)).astype(BF16)
    parts = jnp.concatenate(
        [part0.astype(F32), part1.astype(F32), part2.astype(F32), jnp.zeros((LMAX, width), F32)],
        axis=0,
    ).astype(BF16)
    extra[...] = dot(which, parts)

    for copy in loads[4:]:
        copy.wait()
    hear(0)
    tell(1)

    first = iota((1, 8, chans), 1) == 0
    final = iota((1, 8, chans), 1) == 7

    def gather(lines, a, b):
        return jnp.concatenate([xbuf[t + a, r + b] for t, r in lines], axis=0)

    def convolve(lines, paired, afters=(0, 1, 2), more=False, sums=True):
        count = len(lines)
        window = jnp.concatenate(
            [gather(lines, a, b) for a in afters for b in range(3)], axis=1
        )
        used = slice(afters[0], afters[-1] + 1)
        taps = dot(window, wpair[used].reshape(-1, 2 * chans))
        left = pltpu.roll(taps[:, :chans], 1, 0).reshape(count, cols, chans)
        left = jnp.concatenate([jnp.where(first, 0.0, left[:, :8]), left[:, 8:]], axis=1)
        out = taps[:, chans:].reshape(count, cols, chans) + left
        if paired:
            half = count // 2
            window = jnp.concatenate(
                [gather(lines[::2], a, b) for a in afters for b in range(4)], axis=1
            )
            taps = dot(window, wlast[used].reshape(-1, 2 * chans))
            right = jnp.concatenate(
                [
                    pltpu.roll(
                        taps[:, k * chans : (k + 1) * chans], half * cols - 1, 0
                    ).reshape(half, 1, cols, chans)
                    for k in range(2)
                ],
                axis=1,
            )
        else:
            taps = dot(window, wlast[used, 0:3, :, 0:chans].reshape(-1, chans))
            right = pltpu.roll(taps, count * cols - 1, 0)
        right = right.reshape(count, cols, chans)
        out = out + jnp.concatenate(
            [right[:, :-8], jnp.where(final, 0.0, right[:, -8:])], axis=1
        )
        for t in sorted({t for t, _ in lines}):
            mine = [k for k, line in enumerate(lines) if line[0] == t]
            part = out[mine[0] : mine[-1] + 1]
            if more:
                part = part + hidden[t, pl.ds(lines[mine[0]][1], len(mine))]
            for k in mine:
                hidden[t, lines[k][1]] = part[k - mine[0]]
            if not sums:
                continue
            tiles = part.reshape(len(mine) * cols // 8, 8, chans)
            total, square = jnp.sum(tiles, axis=0), jnp.sum(tiles * tiles, axis=0)
            if not paired:
                total = total + stat[me_h, t, pl.ds(0, 8)]
                square = square + stat[me_h, t, pl.ds(8, 8)]
            stat[me_h, t, pl.ds(0, 8)] = total
            stat[me_h, t, pl.ds(8, 8)] = square

    def clear_rows(at, count):
        @pl.when(me_h == 0)
        def _():
            xbuf[pl.ds(at, count), 0] = jnp.zeros((count, cols, chans), BF16)

        @pl.when(me_h == nh - 1)
        def _():
            xbuf[pl.ds(at, count), rows + 1] = jnp.zeros((count, cols, chans), BF16)

    def stat_copy(t, k):
        return pltpu.make_async_remote_copy(
            src_ref=stat.at[me_h, t], dst_ref=stat.at[me_h, t],
            send_sem=stat_send.at[t, k], recv_sem=stat_recv.at[t, me_h],
            device_id={"tm": me_t, "height": peers[k]}, device_id_type=MESH,
        )

    def stat_arrival(t, k):
        return pltpu.make_async_remote_copy(
            src_ref=stat.at[peers[k], t], dst_ref=stat.at[peers[k], t],
            send_sem=stat_send.at[t, k], recv_sem=stat_recv.at[t, peers[k]],
            device_id={"tm": me_t, "height": peers[k]}, device_id_type=MESH,
        )

    def send_stat(t):
        for k in sorted(range(nh - 1), key=lambda k: -min(k + 1, nh - k - 1)):
            stat_copy(t, k).start()

    group_of = chans // GROUPS
    same = onehot(iota((chans, chans), 0) // group_of == iota((chans, chans), 1) // group_of)
    count = rows * nh * cols * group_of

    def finish(times):
        for t in times:
            for k in range(nh - 1):
                stat_arrival(t, k).wait_recv()
        sums = [
            jnp.sum(jnp.sum(stat[:, t], axis=0).reshape(2, 8, chans), axis=1) for t in times
        ]
        sums = jnp.concatenate(sums + [jnp.zeros((8 - 2 * len(times), chans), F32)], axis=0)
        part0 = sums.astype(BF16).astype(F32)
        part1 = (sums - part0).astype(BF16).astype(F32)
        parts = jnp.concatenate([part0, part1, sums - part0 - part1], axis=0).astype(BF16)
        grouped = dot(parts, same)
        grouped = (grouped[0:8] + grouped[8:16] + grouped[16:24]) / count
        for k, t in enumerate(times):
            average, squares = grouped[2 * k : 2 * k + 1], grouped[2 * k + 1 : 2 * k + 2]
            spread = squares - average * average
            finish_frame(t, average, 0.5 * (lax.rsqrt(spread + EPSILON) * gain[...]))

    def finish_frame(t, average, scale):
        shift = 0.5 * bias[...]

        def act(r, b):
            h = hidden[t, r, pl.ds(b, half_cols, stride=2), :]
            v = (h - average) * scale + shift
            return (v + v * jnp.tanh(v)).astype(BF16)

        merged = jnp.concatenate(
            [
                jnp.concatenate(
                    [act(2 * i + a, b) for a in range(2) for b in range(2)], axis=1
                )
                for i in range(half_rows)
            ],
            axis=0,
        )
        latent = dot(merged, down[...]).astype(BF16)
        latent_out[t] = latent
        at = pl.ds(0 if t == 0 else head + (t - 1) * patches, patches)
        lat[at] = (latent.astype(F32) + extra[at]).astype(BF16)

    interior, edges = range(1, rows - 1), (0, rows - 1)
    for t in range(frames - 1, 1, -1):
        convolve([(t, r) for r in interior], True)
    convolve([(1, r) for r in interior], True, (1, 2), sums=False)
    convolve([(0, r) for r in interior], True, (2,), sums=False)

    @pl.when(has_last)
    def _():
        top.wait_recv()
        corner_up.start()
        bottom.wait_recv()
        corner_down.start()

    to_up.wait_recv()
    to_down.wait_recv()
    hear(1)
    tell(2)
    clear_rows(2, frames)
    convolve([(t, r) for t in range(2, frames) for r in edges], False)
    for t in range(frames - 1, 1, -1):
        send_stat(t)

    @pl.when(has_last)
    def _():
        late.wait_recv()

    @pl.when(jnp.logical_not(has_last))
    def _():
        xbuf[0:2] = jnp.zeros((2, rows + 2, cols, chans), BF16)

    convolve([(1, r) for r in interior], True, (0,), more=True)
    convolve([(0, r) for r in interior], True, (1,), more=True, sums=False)

    @pl.when(has_last)
    def _():
        corner_up.wait_recv()
        corner_down.wait_recv()

    clear_rows(0, 2)
    convolve([(1, r) for r in edges], False)
    send_stat(1)
    convolve([(0, r) for r in edges], False, (1, 2), sums=False)
    hear(2)
    tell(3)

    @pl.when(has_last)
    def _():
        early.wait_recv()

    convolve([(0, r) for r in range(rows)], True, (0,), more=True)
    send_stat(0)
    hear(3)
    tell(4)
    finish(range(frames - 1, 1, -1))
    finish([1])
    rest = pl.ds(head, taken - head)
    total[...] = dot(routes[:, rest], lat[rest])
    finish([0])
    hear(4)
    batch = owners // planes
    turns = [[k for k in order if k < n] for order, n in zip(TURNS, (rows_x, nh, 2))]
    for plane in range(planes):
        z = at_z ^ jnp.where(at_z == 0, planes - 1 - plane, plane)
        here = pl.ds(pl.multiple_of(z * (batch * CAP), batch * CAP), batch * CAP)
        out = dot(routes[here, pl.ds(0, head)], lat[pl.ds(0, head)]) + total[here]
        sides = [
            out[:, k * LANES : (k + 1) * LANES].reshape(batch, CAP, LANES)
            for k in range(width // LANES)
        ]
        pay[pl.ds(z * batch, batch)] = jnp.concatenate(sides, axis=1).astype(BF16)
        for x, h, core in itertools.product(*turns):
            t = (z * rows_x + x) * 2 + core
            k = t * nh + h

            def send():
                pltpu.make_async_remote_copy(
                    src_ref=pay.at[k], dst_ref=arrived.at[me],
                    send_sem=go_sem, recv_sem=come_sem,
                    device_id={"tm": me_t ^ t, "height": me_h ^ h}, device_id_type=MESH,
                ).start()

            if x or h or core:
                send()
            else:
                pl.when(k > 0)(send)
    mine_copy = pltpu.make_async_copy(pay.at[0], arrived.at[me], out_sem)
    mine_copy.start()

    @pl.when(has_next)
    def _():
        for copy in onward:
            copy.wait_send()

    @pl.when(has_last)
    def _():
        corner_up.wait_send()
        corner_down.wait_send()

    to_up.wait_send()
    to_down.wait_send()
    for t in range(frames):
        for k in range(nh - 1):
            stat_copy(t, k).wait_send()
    mine_copy.wait()
    others = pl.ds(0, owners - 1)
    pltpu.make_async_copy(pay.at[others], arrived.at[others], come_sem).wait()
    pltpu.make_async_copy(pay.at[others], arrived.at[others], go_sem).wait()


def compact_kernel(owners, width, arrived, latent_in, routed, latent_out, rows, out, sem):
    latent_copy = pltpu.make_async_copy(latent_in, latent_out, sem.at[0])
    slots = owners * CAP
    block = chunk = min(LANES, slots)
    tall = arrived[...].astype(F32)
    sides = [
        tall[:, k * CAP : (k + 1) * CAP].reshape(slots, LANES) for k in range(width // LANES)
    ]
    rows[...] = jnp.concatenate(sides, axis=1).astype(BF16)
    pick = onehot(iota((8, LANES), 1) == 0)
    lead = dot_t(pick, rows[:, 0:LANES])
    ahead_of = onehot(iota((block, block), 0) < iota((block, block), 1))
    carry = jnp.zeros((8, 1), F32)
    places = []
    for k in range(slots // block):
        valid = jnp.where(lead[:, k * block : (k + 1) * block] < LIMIT, 1.0, 0.0)
        place = dot(valid.astype(BF16), ahead_of) + carry
        carry = carry + jnp.sum(valid, axis=1, keepdims=True)
        places.append(jnp.where(valid > 0.5, place, -1.0)[0:1].astype(jnp.int32))
    latent_copy.start()
    copies = []
    for k in range(slots // chunk):
        at = k * chunk
        line = iota((chunk, block), 0) + at
        chosen = jnp.concatenate(
            [onehot(line == place) for place in places[at // block :]], axis=1
        )
        out[pl.ds(at, chunk)] = dot(chosen, rows[pl.ds(at, slots - at)]).astype(BF16)
        here = pl.ds(at, chunk)
        copies.append(pltpu.make_async_copy(out.at[here], routed.at[here], sem.at[k + 1]))
        copies[-1].start()
    for copy in copies:
        copy.wait()
    latent_copy.wait()


def on_device(
    ntm, nh, video, conv_weight, norm_gain, norm_bias, down_weight, length_table, keep, run_length, owner
):
    frames, rows, cols, chans = video.shape
    width = down_weight.shape[1]
    half_rows, half_cols = rows // 2, cols // 2
    toks = frames * half_rows * half_cols
    owners = ntm * nh
    slots = owners * CAP
    _, taken = heights(half_rows * half_cols, frames)
    ways = (4, 4) if ntm == 32 else (ntm // 2, 1)
    hbm = pl.BlockSpec(memory_space=pltpu.HBM)
    vmem = pl.BlockSpec(memory_space=pltpu.VMEM)
    tiles = CAP * width // LANES
    latent_shape = jax.ShapeDtypeStruct((frames, half_rows * half_cols, width), BF16)
    dma = pltpu.SemaphoreType.DMA
    operands = (
        video,
        conv_weight,
        norm_gain.reshape(1, chans),
        norm_bias.reshape(1, chans),
        down_weight,
        length_table,
        keep,
        run_length,
        owner,
    )
    latent, arrived = pl.pallas_call(
        functools.partial(
            encode_kernel, ntm, nh, (frames, rows, cols, chans, width), ways
        ),
        out_shape=(latent_shape, jax.ShapeDtypeStruct((owners, tiles, LANES), BF16)),
        in_specs=[hbm] * 9,
        out_specs=(vmem, vmem),
        scratch_shapes=[
            pltpu.VMEM((frames + 2, rows + 2, cols, chans), BF16),
            pltpu.VMEM((3, 3, chans, 2 * chans), BF16),
            pltpu.VMEM((3, 4, chans, 2 * chans), BF16),
            pltpu.VMEM((1, chans), F32),
            pltpu.VMEM((1, chans), F32),
            pltpu.VMEM(down_weight.shape, BF16),
            pltpu.VMEM(length_table.shape, F32),
            pltpu.VMEM(keep.shape, jnp.int32),
            pltpu.VMEM(keep.shape, jnp.int32),
            pltpu.VMEM(keep.shape, jnp.int32),
            pltpu.VMEM((frames, rows, cols, chans), F32),
            pltpu.VMEM((nh, frames, 16, chans), F32),
            pltpu.VMEM((slots, taken), BF16),
            pltpu.VMEM((taken, width), F32),
            pltpu.VMEM((taken, width), BF16),
            pltpu.VMEM((slots, width), F32),
            pltpu.VMEM((owners, tiles, LANES), BF16),
            dma((12,)),
            dma((8,)),
            dma((8,)),
            dma((frames, nh - 1)),
            dma((frames, nh)),
            pltpu.SemaphoreType.REGULAR((5,)),
            dma,
            dma,
            dma,
        ],
        compiler_params=pltpu.CompilerParams(
            collective_id=0, has_side_effects=True, vmem_limit_bytes=48 * 1024 * 1024
        ),
        name="encode",
    )(*(pltpu.with_memory_space_constraint(array, pltpu.HBM) for array in operands))
    routed, latent = pl.pallas_call(
        functools.partial(compact_kernel, owners, width),
        out_shape=(jax.ShapeDtypeStruct((slots, width), BF16), latent_shape),
        in_specs=[vmem, hbm],
        out_specs=(hbm, hbm),
        scratch_shapes=[
            pltpu.VMEM((slots, width), BF16),
            pltpu.VMEM((slots, width), BF16),
            dma((9,)),
        ],
        compiler_params=pltpu.CompilerParams(vmem_limit_bytes=48 * 1024 * 1024),
        name="compact",
    )(arrived, latent)
    return latent.reshape(frames, half_rows, half_cols, width), routed


def solution(mesh):
    return jax.shard_map(
        functools.partial(on_device, mesh.shape["tm"], mesh.shape["height"]),
        mesh=mesh,
        in_specs=(
            P("tm", "height", None, None),
            P(),
            P(),
            P(),
            P(),
            P(),
            P("tm", "height", None),
            P("tm", "height", None),
            P("tm", "height", None),
        ),
        out_specs=(P("tm", "height", None, None), P(("tm", "height"), None)),
        check_vma=False,
    )
```

```python
import functools
import itertools

import jax
import jax.numpy as jnp
from jax import lax
from jax.experimental import pallas as pl
from jax.experimental.pallas import tpu as pltpu
from jax.sharding import PartitionSpec as P

GROUPS = 32
LMAX = 8
CAP = 8
EPSILON = 1e-06
LANES = 128
TURNS = ((2, 3, 1, 0), (2, 3, 1, 0), (1, 0))
EMPTY = 2.0**127
LIMIT = 2.0**126
MESH = pl.DeviceIdType.MESH
F32 = jnp.float32
BF16 = jnp.bfloat16


def dot(a, b):
    return jnp.dot(a, b, preferred_element_type=F32)


def dot_t(a, b, precision=None):
    return lax.dot_general(
        a, b, (((1,), (1,)), ((), ())), preferred_element_type=F32, precision=precision
    )


def iota(shape, dim):
    return lax.broadcasted_iota(jnp.int32, shape, dim)


def onehot(mask):
    return jnp.where(mask, 1.0, 0.0).astype(BF16)


def heights(patches, frames):
    head = (patches // LANES + 1) * LANES
    return head, head + -(-(frames - 1) * patches // LANES) * LANES


def encode_kernel(
    ntm, nh, shapes, ways,
    video_in, weight_in, gain_in, bias_in, down_in, table_in, keep_in, run_in, owner_in,
    latent_out, arrived,
    xbuf, wpair, wlast, gain, bias, down, table, keep, run, owner,
    hidden, stat, routes, extra, lat, total, pay,
    in_sem, halo_send, halo_recv, stat_send, stat_recv, ready, out_sem, go_sem, come_sem,
):
    frames, rows, cols, chans, width = shapes
    half_rows, half_cols = rows // 2, cols // 2
    patches = half_rows * half_cols
    toks = frames * patches
    owners = ntm * nh
    slots = owners * CAP
    head, taken = heights(patches, frames)
    me_t, me_h = lax.axis_index("tm"), lax.axis_index("height")
    me = me_t * nh + me_h
    next_t, last_t = lax.rem(me_t + 1, ntm), lax.rem(me_t + ntm - 1, ntm)
    up, down_h = lax.rem(me_h + nh - 1, nh), lax.rem(me_h + 1, nh)
    peers = [lax.rem(me_h + k, nh) for k in range(1, nh)]

    rows_x, planes = ways
    assert owners == 2 * nh * rows_x * planes and all(n & (n - 1) == 0 for n in (nh, *ways))

    even = lax.rem(me_t, 2) == 0
    has_next, has_last = me_t < ntm - 1, me_t > 0

    def signal(semaphore, t, h):
        pl.semaphore_signal(
            semaphore, inc=1, device_id={"tm": t, "height": h}, device_id_type=MESH
        )

    at_x, at_z = lax.rem(me_t // 2, rows_x), me_t // (2 * rows_x)
    first_x = even & (at_x == 0)
    first_z = first_x & (at_z == 0)
    later_x, later_z = even & (at_x > 0), first_x & (at_z > 0)
    to_first_x, to_first_z = me_t - 2 * at_x, 0
    all_x = [me_t + 2 * k for k in range(1, rows_x)]
    all_z = [2 * rows_x * k for k in range(1, planes)]
    relay = [
        (even, [(me_t, h) for h in peers], even, nh - 1),
        (later_x, [(to_first_x, me_h)], first_x, rows_x - 1),
        (later_z, [(to_first_z, me_h)], first_z, planes - 1),
        (first_z, [(t, me_h) for t in all_z], later_z, 1),
        (first_x, [(me_t + k, me_h) for k in range(1, 2 * rows_x)], jnp.logical_not(first_x), 1),
    ]
    barrier = pltpu.get_barrier_semaphore()

    @pl.when(has_last)
    def _():
        signal(barrier, last_t, me_h)

    for h in peers:
        signal(barrier, me_t, h)

    @pl.when(first_x)
    def _():
        for t in all_x:
            signal(barrier, t, me_h)

    @pl.when(first_z)
    def _():
        for t in all_z:
            signal(barrier, t, me_h)

    loads = [
        (keep_in, keep), (run_in, run), (owner_in, owner), (table_in, table),
        (video_in, xbuf.at[pl.ds(2, frames), pl.ds(1, rows)]),
        (weight_in.at[:, :, 0], wpair.at[:, :, :, pl.ds(0, chans)]),
        (weight_in.at[:, :, 1], wpair.at[:, :, :, pl.ds(chans, chans)]),
        (weight_in.at[:, :, 2], wlast.at[:, pl.ds(0, 3), :, pl.ds(0, chans)]),
        (weight_in.at[:, :, 2], wlast.at[:, pl.ds(1, 3), :, pl.ds(chans, chans)]),
        (down_in, down), (gain_in, gain), (bias_in, bias),
    ]
    loads = [
        pltpu.make_async_copy(src, dst, in_sem.at[k]) for k, (src, dst) in enumerate(loads)
    ]
    for copy in loads:
        copy.start()
    wlast[:, 3, :, pl.ds(0, chans)] = jnp.zeros((3, chans, chans), BF16)
    wlast[:, 0, :, pl.ds(chans, chans)] = jnp.zeros((3, chans, chans), BF16)
    awaited = nh - 1 + jnp.where(has_next, 1, 0)
    pl.semaphore_wait(barrier, awaited + jnp.where(later_x | later_z, 1, 0))

    def halo(k, src, dst, t, h):
        return pltpu.make_async_remote_copy(
            src_ref=src, dst_ref=dst, send_sem=halo_send.at[k], recv_sem=halo_recv.at[k],
            device_id={"tm": t, "height": h}, device_id_type=MESH,
        )

    pair = pl.ds(frames - 2, 2)
    inner = pl.ds(1, rows - 2)
    to_up = halo(0, video_in.at[:, 0], xbuf.at[pl.ds(2, frames), rows + 1], me_t, up)
    to_down = halo(1, video_in.at[:, rows - 1], xbuf.at[pl.ds(2, frames), 0], me_t, down_h)
    top = halo(2, video_in.at[pair, 0], xbuf.at[pl.ds(0, 2), 1], next_t, me_h)
    bottom = halo(3, video_in.at[pair, rows - 1], xbuf.at[pl.ds(0, 2), rows], next_t, me_h)
    late = halo(4, video_in.at[frames - 1, inner], xbuf.at[1, pl.ds(2, rows - 2)], next_t, me_h)
    early = halo(5, video_in.at[frames - 2, inner], xbuf.at[0, pl.ds(2, rows - 2)], next_t, me_h)
    corner_up = halo(6, xbuf.at[pl.ds(0, 2), 1], xbuf.at[pl.ds(0, 2), rows + 1], me_t, up)
    corner_down = halo(7, xbuf.at[pl.ds(0, 2), rows], xbuf.at[pl.ds(0, 2), 0], me_t, down_h)
    onward = (top, bottom, late, early)

    @pl.when(has_next)
    def _():
        for copy in onward[:2]:
            copy.start()

    to_up.start()
    to_down.start()

    @pl.when(has_next)
    def _():
        for copy in onward[2:]:
            copy.start()

    def tell(k):
        if k in (0, 4) or (rows_x, planes)[k in (2, 3)] > 1:

            @pl.when(relay[k][0])
            def _():
                for t, h in relay[k][1]:
                    signal(ready.at[k], t, h)

    def hear(k):
        if k in (0, 4) or (rows_x, planes)[k in (2, 3)] > 1:

            @pl.when(relay[k][2])
            def _():
                pl.semaphore_wait(ready.at[k], relay[k][3])

    tell(0)
    for copy in loads[:4]:
        copy.wait()
    def along(pieces, filler):
        row = [pieces[r] for r in range(half_rows)]
        row += [jnp.full((1, head - patches), filler, jnp.int32)]
        row += [pieces[r] for r in range(half_rows, frames * half_rows)]
        row += [jnp.full((1, taken - head - (toks - patches)), filler, jnp.int32)]
        return jnp.concatenate([piece for piece in row if piece.shape[1]], axis=1)

    lines = [(t, slice(r, r + 1)) for t in range(frames) for r in range(half_rows)]
    place = []
    for t, r in lines:
        place.append(jnp.where(keep[t, r] == 1, owner[t, r] ^ me, -1))
    place = along(place, -1)
    length = along([run[t, r] - 1 for t, r in lines], -1)
    member = iota((owners, taken), 0) == place
    before_lane = onehot(iota((LANES, LANES), 0) < iota((LANES, LANES), 1))
    kept = jnp.zeros((owners, 1), F32)
    for k in range(taken // LANES):
        at = slice(k * LANES, (k + 1) * LANES)
        block = jnp.where(member[:, at], 1.0, 0.0)
        ahead = dot(block.astype(BF16), before_lane) + kept
        kept = kept + jnp.sum(block, axis=1, keepdims=True)
        rank = jnp.sum(ahead * block, axis=0, keepdims=True).astype(jnp.int32)
        slot = jnp.where(place[:, at] < 0, -1, place[:, at] * CAP + rank)
        chosen = iota((slots, LANES), 0) == slot
        if k == patches // LANES:
            partly = chosen
        else:
            routes[:, at] = onehot(chosen)
    at = slice(patches // LANES * LANES, (patches // LANES + 1) * LANES)
    unused = iota((owners, CAP, LANES), 1).astype(F32) >= kept.reshape(owners, 1, 1)
    mark = unused & (iota((owners, CAP, LANES), 2) == patches % LANES)
    routes[:, at] = jnp.maximum(
        onehot(partly).astype(F32), jnp.where(mark, 1.0, 0.0).reshape(slots, LANES)
    ).astype(BF16)
    lat[pl.ds(patches, head - patches)] = jnp.where(
        iota((head - patches, width), 0) == 0, EMPTY, 0.0
    ).astype(BF16)
    if taken > head + toks - patches:
        tail = taken - head - (toks - patches)
        lat[pl.ds(taken - tail, tail)] = jnp.zeros((tail, width), BF16)
    row_of = iota((4 * LMAX, taken), 0)
    which = (lax.rem(row_of, LMAX) == length) & (row_of < 3 * LMAX)
    which = jnp.where(which, 1.0, 0.0).T.astype(BF16)
    part0 = table[...].astype(BF16)
    rest = table[...] - part0.astype(F32)
    part1 = rest.astype(BF16)
    part2 = (rest - part1.astype(F32)).astype(BF16)
    parts = jnp.concatenate(
        [part0.astype(F32), part1.astype(F32), part2.astype(F32), jnp.zeros((LMAX, width), F32)],
        axis=0,
    ).astype(BF16)
    extra[...] = dot(which, parts)

    for copy in loads[4:]:
        copy.wait()
    hear(0)
    tell(1)

    first = iota((1, 8, chans), 1) == 0
    final = iota((1, 8, chans), 1) == 7

    def gather(lines, a, b):
        return jnp.concatenate([xbuf[t + a, r + b] for t, r in lines], axis=0)

    def convolve(lines, paired, afters=(0, 1, 2), more=False, sums=True):
        count = len(lines)
        window = jnp.concatenate(
            [gather(lines, a, b) for a in afters for b in range(3)], axis=1
        )
        used = slice(afters[0], afters[-1] + 1)
        taps = dot(window, wpair[used].reshape(-1, 2 * chans))
        left = pltpu.roll(taps[:, :chans], 1, 0).reshape(count, cols, chans)
        left = jnp.concatenate([jnp.where(first, 0.0, left[:, :8]), left[:, 8:]], axis=1)
        out = taps[:, chans:].reshape(count, cols, chans) + left
        if paired:
            half = count // 2
            window = jnp.concatenate(
                [gather(lines[::2], a, b) for a in afters for b in range(4)], axis=1
            )
            taps = dot(window, wlast[used].reshape(-1, 2 * chans))
            right = jnp.concatenate(
                [
                    pltpu.roll(
                        taps[:, k * chans : (k + 1) * chans], half * cols - 1, 0
                    ).reshape(half, 1, cols, chans)
                    for k in range(2)
                ],
                axis=1,
            )
        else:
            taps = dot(window, wlast[used, 0:3, :, 0:chans].reshape(-1, chans))
            right = pltpu.roll(taps, count * cols - 1, 0)
        right = right.reshape(count, cols, chans)
        out = out + jnp.concatenate(
            [right[:, :-8], jnp.where(final, 0.0, right[:, -8:])], axis=1
        )
        for t in sorted({t for t, _ in lines}):
            mine = [k for k, line in enumerate(lines) if line[0] == t]
            part = out[mine[0] : mine[-1] + 1]
            if more:
                part = part + hidden[t, pl.ds(lines[mine[0]][1], len(mine))]
            for k in mine:
                hidden[t, lines[k][1]] = part[k - mine[0]]
            if not sums:
                continue
            tiles = part.reshape(len(mine) * cols // 8, 8, chans)
            total, square = jnp.sum(tiles, axis=0), jnp.sum(tiles * tiles, axis=0)
            if not paired:
                total = total + stat[me_h, t, pl.ds(0, 8)]
                square = square + stat[me_h, t, pl.ds(8, 8)]
            stat[me_h, t, pl.ds(0, 8)] = total
            stat[me_h, t, pl.ds(8, 8)] = square

    def clear_rows(at, count):
        @pl.when(me_h == 0)
        def _():
            xbuf[pl.ds(at, count), 0] = jnp.zeros((count, cols, chans), BF16)

        @pl.when(me_h == nh - 1)
        def _():
            xbuf[pl.ds(at, count), rows + 1] = jnp.zeros((count, cols, chans), BF16)

    def stat_copy(t, k):
        return pltpu.make_async_remote_copy(
            src_ref=stat.at[me_h, t], dst_ref=stat.at[me_h, t],
            send_sem=stat_send.at[t, k], recv_sem=stat_recv.at[t, me_h],
            device_id={"tm": me_t, "height": peers[k]}, device_id_type=MESH,
        )

    def stat_arrival(t, k):
        return pltpu.make_async_remote_copy(
            src_ref=stat.at[peers[k], t], dst_ref=stat.at[peers[k], t],
            send_sem=stat_send.at[t, k], recv_sem=stat_recv.at[t, peers[k]],
            device_id={"tm": me_t, "height": peers[k]}, device_id_type=MESH,
        )

    def send_stat(t):
        for k in sorted(range(nh - 1), key=lambda k: -min(k + 1, nh - k - 1)):
            stat_copy(t, k).start()

    group_of = chans // GROUPS
    same = onehot(iota((chans, chans), 0) // group_of == iota((chans, chans), 1) // group_of)
    count = rows * nh * cols * group_of

    def finish(times):
        for t in times:
            for k in range(nh - 1):
                stat_arrival(t, k).wait_recv()
        sums = [
            jnp.sum(jnp.sum(stat[:, t], axis=0).reshape(2, 8, chans), axis=1) for t in times
        ]
        sums = jnp.concatenate(sums + [jnp.zeros((8 - 2 * len(times), chans), F32)], axis=0)
        part0 = sums.astype(BF16).astype(F32)
        part1 = (sums - part0).astype(BF16).astype(F32)
        parts = jnp.concatenate([part0, part1, sums - part0 - part1], axis=0).astype(BF16)
        grouped = dot(parts, same)
        grouped = (grouped[0:8] + grouped[8:16] + grouped[16:24]) / count
        for k, t in enumerate(times):
            average, squares = grouped[2 * k : 2 * k + 1], grouped[2 * k + 1 : 2 * k + 2]
            spread = squares - average * average
            finish_frame(t, average, 0.5 * (lax.rsqrt(spread + EPSILON) * gain[...]))

    def finish_frame(t, average, scale):
        shift = 0.5 * bias[...]

        def act(r, b):
            h = hidden[t, r, pl.ds(b, half_cols, stride=2), :]
            v = (h - average) * scale + shift
            return (v + v * jnp.tanh(v)).astype(BF16)

        merged = jnp.concatenate(
            [
                jnp.concatenate(
                    [act(2 * i + a, b) for a in range(2) for b in range(2)], axis=1
                )
                for i in range(half_rows)
            ],
            axis=0,
        )
        latent = dot(merged, down[...]).astype(BF16)
        latent_out[t] = latent
        at = pl.ds(0 if t == 0 else head + (t - 1) * patches, patches)
        lat[at] = (latent.astype(F32) + extra[at]).astype(BF16)

    interior, edges = range(1, rows - 1), (0, rows - 1)
    for t in range(frames - 1, 1, -1):
        convolve([(t, r) for r in interior], True)
    convolve([(1, r) for r in interior], True, (1, 2), sums=False)
    convolve([(0, r) for r in interior], True, (2,), sums=False)

    @pl.when(has_last)
    def _():
        top.wait_recv()
        corner_up.start()
        bottom.wait_recv()
        corner_down.start()

    to_up.wait_recv()
    to_down.wait_recv()
    hear(1)
    tell(2)
    clear_rows(2, frames)
    convolve([(t, r) for t in range(2, frames) for r in edges], False)
    for t in range(frames - 1, 1, -1):
        send_stat(t)

    @pl.when(has_last)
    def _():
        late.wait_recv()

    @pl.when(jnp.logical_not(has_last))
    def _():
        xbuf[0:2] = jnp.zeros((2, rows + 2, cols, chans), BF16)

    convolve([(1, r) for r in interior], True, (0,), more=True)
    convolve([(0, r) for r in interior], True, (1,), more=True, sums=False)

    @pl.when(has_last)
    def _():
        corner_up.wait_recv()
        corner_down.wait_recv()

    clear_rows(0, 2)
    convolve([(1, r) for r in edges], False)
    send_stat(1)
    convolve([(0, r) for r in edges], False, (1, 2), sums=False)
    hear(2)
    tell(3)

    @pl.when(has_last)
    def _():
        early.wait_recv()

    convolve([(0, r) for r in range(rows)], True, (0,), more=True)
    send_stat(0)
    hear(3)
    tell(4)
    finish(range(frames - 1, 1, -1))
    finish([1])
    rest = pl.ds(head, taken - head)
    total[...] = dot(routes[:, rest], lat[rest])
    finish([0])
    hear(4)
    batch = owners // planes
    turns = [[k for k in order if k < n] for order, n in zip(TURNS, (rows_x, nh, 2))]
    for plane in range(planes):
        z = at_z ^ plane
        here = pl.ds(pl.multiple_of(z * (batch * CAP), batch * CAP), batch * CAP)
        out = dot(routes[here, pl.ds(0, head)], lat[pl.ds(0, head)]) + total[here]
        sides = [
            out[:, k * LANES : (k + 1) * LANES].reshape(batch, CAP, LANES)
            for k in range(width // LANES)
        ]
        pay[pl.ds(z * batch, batch)] = jnp.concatenate(sides, axis=1).astype(BF16)
        for core, x, h in itertools.product(turns[2], turns[0], turns[1]):
            t = (z * rows_x + x) * 2 + core
            k = t * nh + h

            def send():
                pltpu.make_async_remote_copy(
                    src_ref=pay.at[k], dst_ref=arrived.at[me],
                    send_sem=go_sem, recv_sem=come_sem,
                    device_id={"tm": me_t ^ t, "height": me_h ^ h}, device_id_type=MESH,
                ).start()

            if x or h or core:
                send()
            else:
                pl.when(k > 0)(send)
    mine_copy = pltpu.make_async_copy(pay.at[0], arrived.at[me], out_sem)
    mine_copy.start()

    @pl.when(has_next)
    def _():
        for copy in onward:
            copy.wait_send()

    @pl.when(has_last)
    def _():
        corner_up.wait_send()
        corner_down.wait_send()

    to_up.wait_send()
    to_down.wait_send()
    for t in range(frames):
        for k in range(nh - 1):
            stat_copy(t, k).wait_send()
    mine_copy.wait()
    others = pl.ds(0, owners - 1)
    pltpu.make_async_copy(pay.at[others], arrived.at[others], come_sem).wait()
    pltpu.make_async_copy(pay.at[others], arrived.at[others], go_sem).wait()


def compact_kernel(owners, width, arrived, latent_in, routed, latent_out, rows, out, sem):
    latent_copy = pltpu.make_async_copy(latent_in, latent_out, sem.at[0])
    slots = owners * CAP
    block, chunk = min(LANES, slots), min(2 * LANES, slots)
    tall = arrived[...].astype(F32)
    sides = [
        tall[:, k * CAP : (k + 1) * CAP].reshape(slots, LANES) for k in range(width // LANES)
    ]
    rows[...] = jnp.concatenate(sides, axis=1).astype(BF16)
    pick = onehot(iota((8, LANES), 1) == 0)
    lead = dot_t(pick, rows[:, 0:LANES])
    ahead_of = onehot(iota((block, block), 0) < iota((block, block), 1))
    carry = jnp.zeros((8, 1), F32)
    places = []
    for k in range(slots // block):
        valid = jnp.where(lead[:, k * block : (k + 1) * block] < LIMIT, 1.0, 0.0)
        place = dot(valid.astype(BF16), ahead_of) + carry
        carry = carry + jnp.sum(valid, axis=1, keepdims=True)
        places.append(jnp.where(valid > 0.5, place, -1.0)[0:1].astype(jnp.int32))
    latent_copy.start()
    copies = []
    for k in range(slots // chunk):
        at = k * chunk
        line = iota((chunk, block), 0) + at
        chosen = jnp.concatenate(
            [onehot(line == place) for place in places[at // block :]], axis=1
        )
        out[pl.ds(at, chunk)] = dot(chosen, rows[pl.ds(at, slots - at)]).astype(BF16)
        here = pl.ds(at, chunk)
        copies.append(pltpu.make_async_copy(out.at[here], routed.at[here], sem.at[k + 1]))
        copies[-1].start()
    for copy in copies:
        copy.wait()
    latent_copy.wait()


def on_device(
    ntm, nh, video, conv_weight, norm_gain, norm_bias, down_weight, length_table, keep, run_length, owner
):
    frames, rows, cols, chans = video.shape
    width = down_weight.shape[1]
    half_rows, half_cols = rows // 2, cols // 2
    toks = frames * half_rows * half_cols
    owners = ntm * nh
    slots = owners * CAP
    _, taken = heights(half_rows * half_cols, frames)
    ways = (4, 4) if ntm == 32 else (ntm // 2, 1)
    hbm = pl.BlockSpec(memory_space=pltpu.HBM)
    vmem = pl.BlockSpec(memory_space=pltpu.VMEM)
    tiles = CAP * width // LANES
    latent_shape = jax.ShapeDtypeStruct((frames, half_rows * half_cols, width), BF16)
    dma = pltpu.SemaphoreType.DMA
    operands = (
        video,
        conv_weight,
        norm_gain.reshape(1, chans),
        norm_bias.reshape(1, chans),
        down_weight,
        length_table,
        keep,
        run_length,
        owner,
    )
    latent, arrived = pl.pallas_call(
        functools.partial(
            encode_kernel, ntm, nh, (frames, rows, cols, chans, width), ways
        ),
        out_shape=(latent_shape, jax.ShapeDtypeStruct((owners, tiles, LANES), BF16)),
        in_specs=[hbm] * 9,
        out_specs=(vmem, vmem),
        scratch_shapes=[
            pltpu.VMEM((frames + 2, rows + 2, cols, chans), BF16),
            pltpu.VMEM((3, 3, chans, 2 * chans), BF16),
            pltpu.VMEM((3, 4, chans, 2 * chans), BF16),
            pltpu.VMEM((1, chans), F32),
            pltpu.VMEM((1, chans), F32),
            pltpu.VMEM(down_weight.shape, BF16),
            pltpu.VMEM(length_table.shape, F32),
            pltpu.VMEM(keep.shape, jnp.int32),
            pltpu.VMEM(keep.shape, jnp.int32),
            pltpu.VMEM(keep.shape, jnp.int32),
            pltpu.VMEM((frames, rows, cols, chans), F32),
            pltpu.VMEM((nh, frames, 16, chans), F32),
            pltpu.VMEM((slots, taken), BF16),
            pltpu.VMEM((taken, width), F32),
            pltpu.VMEM((taken, width), BF16),
            pltpu.VMEM((slots, width), F32),
            pltpu.VMEM((owners, tiles, LANES), BF16),
            dma((12,)),
            dma((8,)),
            dma((8,)),
            dma((frames, nh - 1)),
            dma((frames, nh)),
            pltpu.SemaphoreType.REGULAR((5,)),
            dma,
            dma,
            dma,
        ],
        compiler_params=pltpu.CompilerParams(
            collective_id=0, has_side_effects=True, vmem_limit_bytes=48 * 1024 * 1024
        ),
        name="encode",
    )(*(pltpu.with_memory_space_constraint(array, pltpu.HBM) for array in operands))
    routed, latent = pl.pallas_call(
        functools.partial(compact_kernel, owners, width),
        out_shape=(jax.ShapeDtypeStruct((slots, width), BF16), latent_shape),
        in_specs=[vmem, hbm],
        out_specs=(hbm, hbm),
        scratch_shapes=[
            pltpu.VMEM((slots, width), BF16),
            pltpu.VMEM((slots, width), BF16),
            dma((5,)),
        ],
        compiler_params=pltpu.CompilerParams(vmem_limit_bytes=48 * 1024 * 1024),
        name="compact",
    )(arrived, latent)
    return latent.reshape(frames, half_rows, half_cols, width), routed


def solution(mesh):
    return jax.shard_map(
        functools.partial(on_device, mesh.shape["tm"], mesh.shape["height"]),
        mesh=mesh,
        in_specs=(
            P("tm", "height", None, None),
            P(),
            P(),
            P(),
            P(),
            P(),
            P("tm", "height", None),
            P("tm", "height", None),
            P("tm", "height", None),
        ),
        out_specs=(P("tm", "height", None, None), P(("tm", "height"), None)),
        check_vma=False,
    )
```
